128 devices in a mesh: node: 32 (over z, y, core), head: 4 (over x).
Axes of the slice: x: 4, y: 4, z: 4, core: 2. Of those that a mesh axis runs over, the one named last changes fastest.
Arguments:
- queries: bfloat16 [8192, 8, 8, 128], P('node', None, 'head')
- keys: bfloat16 [8192, 8, 128], P('node', 'head')
- values: bfloat16 [8192, 8, 128], P('node', 'head'), may hold values from -6 to 6
- grad_out: bfloat16 [8192, 8, 8, 128], P('node', None, 'head'), may hold values from -6 to 6
- parents: int32 [32], replicated, may hold values from -1 to 0, as said below
- node_lengths: int32 [32], replicated, may hold values from 64 to 256
Outputs:
- attended: bfloat16 [8192, 8, 8, 128], P('node', None, 'head')
- grad_queries: bfloat16 [8192, 8, 8, 128], P('node', None, 'head')
- grad_keys: bfloat16 [8192, 8, 128], P('node', 'head')
- grad_values: bfloat16 [8192, 8, 128], P('node', 'head')
The draws below stay inside these ranges and needn't reach their ends.
Inputs may be any that keep to these rules, and one draw needn't show every extreme that they name: `parents`: nodes on node-axis indices p with p % 4 == 0 are roots (-1); every other node has parent slot 0 (there is one node per index of the node axis), so a tree spans 4 consecutive indices of the node axis.
All inputs are finite; a program needn't handle non-finite values.
Results may differ from the reference program's by a relative error of at most 0.0067.
Values may be sent and summed in bfloat16 or wider, within the bound.
A program may use at most 128 MiB of HBM per device.

```python
import jax
import jax.numpy as jnp
from jax import lax

NODE_DEV = 1
NODE_TOK = 256
LEVELS = 4
KVH = 8
GROUP = 8
HD = 128
NODES = 32
TOKENS = 8192


def shared_keys(key):
    return jax.random.normal(jax.random.fold_in(key, 101), (TOKENS, KVH, HD), jnp.float32)


def draw_keys(key, part):
    base_keys = shared_keys(key)
    return base_keys.astype(jnp.bfloat16)


def draw_queries(key, part):
    key = jax.random.fold_in(key, 1)
    drawn = jax.random.normal(key, (TOKENS, KVH, GROUP, HD), jnp.float32)
    return drawn.astype(jnp.bfloat16)


def draw_parents(key, part):
    key = jax.random.fold_in(key, 3)
    node_ids = jnp.arange(NODES, dtype=jnp.int32)
    devices = node_ids // NODE_DEV
    favored = jax.random.randint(jax.random.fold_in(key, 1), (NODES // NODE_DEV,), 0, NODE_DEV)[devices]
    coin = jax.random.randint(jax.random.fold_in(key, 2), (NODES,), 0, 2)
    spread = jax.random.randint(jax.random.fold_in(key, 3), (NODES,), 0, NODE_DEV)
    slots = jnp.where(coin == 0, favored, spread)
    slots = jnp.where(devices % LEVELS == 0, -1, slots)
    slots = slots.at[NODE_DEV].set(NODE_DEV - 1)
    return slots.astype(jnp.int32)


def draw_node_lengths(key, part):
    key = jax.random.fold_in(key, 4)
    lengths = jax.random.randint(key, (NODES,), NODE_TOK // 4, NODE_TOK + 1)
    lengths = lengths.at[0].set(NODE_TOK)
    lengths = lengths.at[1].set(NODE_TOK // 4)
    return lengths.astype(jnp.int32)


def shard_levels(own_key, shape, shards, smallest, largest):
    def one(position, blocks):
        heights = jax.random.uniform(jax.random.fold_in(jax.random.fold_in(own_key, 6), position), (blocks,), jnp.float32, smallest / len(shards), largest / len(shards))
        return jnp.repeat(jnp.exp(heights), shape[position] // blocks).reshape((-1,) + (1,) * (len(shape) - position - 1))

    factor_of = one(*shards[0])
    for cut in shards[1:]:
        factor_of = factor_of * one(*cut)
    return factor_of


def centred(rng, shape, scale, reach, cuts=(), held_as=jnp.bfloat16):
    loudness = shard_levels(rng, shape, cuts, -0.22, 0.18) if cuts else 1.0
    values = jax.random.normal(rng, shape, jnp.float32) * scale * loudness
    return jnp.minimum(jnp.maximum(values, -reach), reach).astype(held_as)


def setup_inputs(seed: int = 0) -> dict:
    arg_keys = jax.random.split(jax.random.key(seed), 7)
    queries = draw_queries(jax.random.fold_in(arg_keys[6], 71), 0)
    keys = draw_keys(jax.random.fold_in(arg_keys[6], 71), 0)
    values = centred(arg_keys[2], (TOKENS, KVH, HD), 1.0, 6.0, ((0, 32), (1, 4)))
    grad_out = centred(arg_keys[3], (TOKENS, KVH, GROUP, HD), 1.0, 6.0, ((0, 32), (2, 4)))
    parents = draw_parents(jax.random.fold_in(arg_keys[6], 71), 0)
    node_lengths = draw_node_lengths(jax.random.fold_in(arg_keys[6], 71), 0)
    return {"queries": queries, "keys": keys, "values": values, "grad_out": grad_out, "parents": parents, "node_lengths": node_lengths}


def ancestry(parents):
    node_ids = jnp.arange(NODES, dtype=jnp.int32)
    devices = node_ids // NODE_DEV
    current = node_ids
    present = jnp.ones((NODES,), dtype=bool)
    id_list = []
    present_list = []
    for distance in range(LEVELS):
        id_list.append(current)
        present_list.append(present)
        parent_slot = jnp.take(parents, jnp.clip(current, 0, NODES - 1))
        present = present & (parent_slot >= 0)
        current = ((devices - distance - 1) * NODE_DEV + jnp.maximum(parent_slot, 0)).astype(jnp.int32)
    return jnp.stack(id_list, 1), jnp.stack(present_list, 1)


def visible_keys(present, lengths):
    rows = jnp.arange(NODE_TOK, dtype=jnp.int32)[:, None]
    cols = jnp.arange(NODE_TOK, dtype=jnp.int32)[None, :]
    depth = jnp.arange(LEVELS, dtype=jnp.int32)[:, None, None]
    allowed = present[:, None, None] & (cols[None] < lengths[:, None, None]) & ((depth > 0) | (cols <= rows)[None])
    return jnp.transpose(allowed, (1, 0, 2)).reshape(NODE_TOK, LEVELS * NODE_TOK)


def attend(node_query_rows, ancestor_key_rows, ancestor_value_rows, node_gradient, allowed):
    logit_scale = HD ** -0.5
    query_full = node_query_rows.astype(jnp.float32)
    key_full = ancestor_key_rows.astype(jnp.float32)
    value_full = ancestor_value_rows.astype(jnp.float32)
    gradient_full = node_gradient.astype(jnp.float32)
    attention_logits = jnp.einsum('nujq,euq->ujne', query_full, key_full) * logit_scale
    attention_logits = jnp.where(allowed, attention_logits, -jnp.inf)
    top_score = jnp.max(attention_logits, -1, keepdims=True)
    expo = jnp.exp(attention_logits - top_score)
    weights = expo / jnp.sum(expo, -1, keepdims=True)
    weight_reduced = weights.astype(jnp.bfloat16)
    attention_output = jnp.einsum('oibh,hom->boim', weight_reduced.astype(jnp.float32), value_full)
    weight_gradient = jnp.einsum('nujq,euq->ujne', gradient_full, value_full)
    row_dot = jnp.transpose(jnp.sum(gradient_full * attention_output, -1), (1, 2, 0))[..., None]
    score_gradient = (weights * (weight_gradient - row_dot)).astype(jnp.bfloat16).astype(jnp.float32)
    query_gradient = (logit_scale * jnp.einsum('oibh,hom->boim', score_gradient, key_full)).astype(jnp.bfloat16)
    key_gradient = logit_scale * jnp.einsum('xukz,kxui->zxi', score_gradient, query_full)
    value_gradient = jnp.einsum('xukz,kxui->zxi', weight_reduced.astype(jnp.float32), gradient_full)
    return attention_output.astype(jnp.bfloat16), query_gradient, jnp.stack([key_gradient, value_gradient])


def reference(queries, keys, values, grad_out, parents, node_lengths):
    source_ids, present = ancestry(parents)
    clipped = jnp.clip(source_ids, 0, NODES - 1).astype(jnp.int32)
    lengths_up = jnp.take(node_lengths, clipped)
    query_nodes = queries.reshape(NODES, NODE_TOK, KVH, GROUP, HD)
    grad_nodes = grad_out.reshape(NODES, NODE_TOK, KVH, GROUP, HD)
    key_nodes = keys.reshape(NODES, NODE_TOK, KVH, HD)
    value_nodes = values.reshape(NODES, NODE_TOK, KVH, HD)

    def step(running, node_index):
        chain = clipped[node_index]
        ancestor_key_rows = jnp.take(key_nodes, chain, axis=0).reshape(LEVELS * NODE_TOK, KVH, HD)
        ancestor_value_rows = jnp.take(value_nodes, chain, axis=0).reshape(LEVELS * NODE_TOK, KVH, HD)
        allowed = visible_keys(present[node_index], lengths_up[node_index])
        attention_output, query_gradient, grads = attend(query_nodes[node_index], ancestor_key_rows, ancestor_value_rows, grad_nodes[node_index], allowed)
        running = running.at[:, chain].add(grads.reshape(2, LEVELS, NODE_TOK, KVH, HD))
        return running, (attention_output, query_gradient)

    init = jnp.zeros((2, NODES, NODE_TOK, KVH, HD), jnp.float32)
    summed, (outputs, grad_queries) = lax.scan(step, init, jnp.arange(NODES, dtype=jnp.int32))
    attended = outputs.reshape(TOKENS, KVH, GROUP, HD)
    grad_q = grad_queries.reshape(TOKENS, KVH, GROUP, HD)
    grad_keys = summed[0].reshape(TOKENS, KVH, HD).astype(jnp.bfloat16)
    grad_values = summed[1].reshape(TOKENS, KVH, HD).astype(jnp.bfloat16)
    return (attended, grad_q, grad_keys, grad_values)
```

```python
import functools
import math

import jax
import jax.numpy as jnp
from jax import lax
from jax.experimental import pallas as pl
from jax.experimental.pallas import tpu as pltpu
from jax.sharding import PartitionSpec as P

MESH = pl.DeviceIdType.MESH
TOK = 256
LEVELS = 4
KVH = 8
HD = 128
ROWS = 512
SCALE = HD ** -0.5
SCORE_SCALE = SCALE * math.log2(math.e)

UNITS = ((0, 0), (1, 1), (3, 0), (2, 0), (2, 1), (1, 0), (3, 1), (0, 1))
ORDER = (0, 1, 2, 3, 4, 5, 6, 7)


def nt(a, b):
    return lax.dot_general(a, b, (((1,), (1,)), ((), ())), preferred_element_type=jnp.float32)


def tn(a, b):
    return lax.dot_general(a, b, (((0,), (0,)), ((), ())), preferred_element_type=jnp.float32)


def nn(a, b):
    return lax.dot_general(a, b, (((1,), (0,)), ((), ())), preferred_element_type=jnp.float32)


def when(cond, fn):
    if cond is None:
        fn()
    else:
        pl.when(cond)(fn)


def table(step, values):
    picked = jnp.int32(values[0])
    for at in range(1, len(values)):
        picked = jnp.where(step == at, jnp.int32(values[at]), picked)
    return picked


def kernel(
    q_ref, g_ref, k_ref, v_ref, len_ref,
    o_ref, dq_ref, dk_ref, dv_ref,
    kv, qh, gh, wide_o, wide_q, pair, score, part,
    sib_out, sib_in, x_out, x_in, transit, y_out, y_in,
    in_sem, out_sem, sib_sem, x_sem, transit_sem, y_sem,
):
    p = lax.axis_index("node")
    x = lax.axis_index("head")
    level = lax.rem(p, LEVELS)
    odd = lax.rem(p, 2)
    xp = lax.rem(x + 1, 4)
    xm = lax.rem(x + 3, 4)
    upper = level >= 2
    even = odd == 0
    to_xp = (p, xp)
    to_xm = (p, xm)
    to_sib = (p + 1 - 2 * odd, x)
    to_y = (p + 2 - 4 * (level // 2), x)

    def head_of(unit):
        hop, at = UNITS[unit]
        return 2 * lax.rem(x + hop, 4) + at

    sends = {}

    def define(name, cond, make):
        sends[name] = (cond, make, len(sends))

    def start(name):
        cond, make, at = sends[name]
        when(cond, lambda: make(at).start())

    def kv_copy(lev, head, unit, device):
        def make(at):
            return pltpu.make_async_remote_copy(
                src_ref=kv.at[lev, head], dst_ref=kv.at[lev, head],
                send_sem=out_sem.at[at], recv_sem=in_sem.at[lev, unit],
                device_id=device, device_id_type=MESH)
        return make

    def plain_copy(src, dst, sem, device):
        def make(at):
            return pltpu.make_async_remote_copy(
                src_ref=src, dst_ref=dst, send_sem=out_sem.at[at], recv_sem=sem,
                device_id=device, device_id_type=MESH)
        return make

    up2 = jnp.maximum(level - 2, 0)
    lev_of = (level, up2)
    cond_of = (None, upper)
    for a in range(2):
        lev, cond = lev_of[a], cond_of[a]
        define(("own", a, 1), cond, kv_copy(lev, head_of(7), 1, to_xm))
        define(("own", a, 2), cond, kv_copy(lev, head_of(0), 2, to_xp))
        define(("own", a, 5), cond, kv_copy(lev, head_of(0), 5, to_xm))
        define(("own", a, 6), cond, kv_copy(lev, head_of(7), 6, to_xp))
        define(("far", a, 3), cond, kv_copy(lev, head_of(2), 3, to_xp))
        define(("far", a, 4), cond, kv_copy(lev, head_of(1), 4, to_xm))
        for unit in range(8):
            define(("sib", a, unit), even if a == 0 else upper,
                   kv_copy(lev, head_of(unit), unit, to_sib))
    for unit in (0, 7):
        define(("up", unit), level < 2, kv_copy(level, head_of(unit), unit, to_y))
    for unit in range(8):
        define(("part", unit, 0), level >= 1,
               plain_copy(sib_out.at[unit, 0], sib_in.at[unit, 0], sib_sem.at[unit, 0], to_sib))
        define(("part", unit, 1), level == 3,
               plain_copy(sib_out.at[unit, 1], sib_in.at[unit, 1], sib_sem.at[unit, 1], to_sib))
    x_plan = {
        1: (to_xp, lambda a: (x_in.at[a, 1, 0], x_sem.at[a, 1, 0])),
        2: (to_xm, lambda a: (x_in.at[a, 0, 1], x_sem.at[a, 0, 1])),
        3: (to_xp, lambda a: (transit.at[a, 0], transit_sem.at[a, 0])),
        4: (to_xm, lambda a: (transit.at[a, 1], transit_sem.at[a, 1])),
        5: (to_xp, lambda a: (x_in.at[a, 0, 0], x_sem.at[a, 0, 0])),
        6: (to_xm, lambda a: (x_in.at[a, 1, 1], x_sem.at[a, 1, 1])),
    }
    for unit, (device, there) in x_plan.items():
        for a in range(2):
            dst, sem = there(a)
            define(("x", unit, a), cond_of[a], plain_copy(x_out.at[a, unit - 1], dst, sem, device))
    for at in range(2):
        define(("down", at), upper, plain_copy(y_out.at[at], y_in.at[at], y_sem.at[at], to_y))

    def wait_in(dst, sem):
        pltpu.make_async_remote_copy(
            src_ref=dst, dst_ref=dst, send_sem=out_sem.at[0], recv_sem=sem,
            device_id=to_sib, device_id_type=MESH).wait_recv()

    def wait_kv(lev, unit):
        wait_in(kv.at[lev, head_of(unit)], in_sem.at[lev, unit])

    def arrive(a, unit):
        def body():
            wait_kv(lev_of[a], unit)
            if a == 1 and unit == 0:
                start(("own", 1, 2))
                start(("own", 1, 5))
            if a == 1 and unit == 7:
                start(("own", 1, 1))
                start(("own", 1, 6))
            if unit == 2:
                start(("far", a, 3))
            if unit == 1:
                start(("far", a, 4))
            start(("sib", a, unit))
        when(cond_of[a], body)

    def from_sibling(unit):
        pl.when(level >= 1)(lambda: wait_kv(jnp.maximum(level - 1, 0), unit))
        pl.when(level == 3)(lambda: wait_kv(jnp.int32(0), unit))

    barrier = pltpu.get_barrier_semaphore()
    for device in (to_xp, to_xm, to_sib, to_y):
        pl.semaphore_signal(barrier, inc=1, device_id=device, device_id_type=MESH)

    for which, ref in ((0, k_ref), (1, v_ref)):
        pair[...] = ref[...].astype(jnp.float32)
        for at in range(2):
            kv[level, 2 * x + at, which] = pair[pl.ds(at, TOK, stride=2), :].astype(jnp.bfloat16)
    pl.semaphore_wait(barrier, 4)

    start(("own", 0, 1))
    start(("own", 0, 2))
    start(("up", 0))
    start(("up", 7))
    start(("sib", 0, 0))
    start(("sib", 0, 7))
    start(("own", 0, 5))
    start(("own", 0, 6))

    for lev in range(1, LEVELS):
        def blank(lev=lev):
            kv[lev] = jnp.zeros((KVH, 2, TOK, HD), jnp.bfloat16)
        pl.when(level < lev)(blank)

    for src, wide, dst in ((q_ref, wide_o, qh), (g_ref, wide_q, gh)):
        wide[...] = src[...].astype(jnp.float32)
        for head in range(KVH):
            for r in range(2):
                dst[head, r * TOK:(r + 1) * TOK, :] = (
                    wide[pl.ds(2 * head + r, TOK, stride=16), :].astype(jnp.bfloat16))

    lengths = []
    for k in range(LEVELS):
        real = len_ref[jnp.maximum(p - k, 0)]
        lengths.append(jnp.where(level >= k, real, 0))

    def compute(step):
        hop = table(step, [UNITS[u][0] for u in ORDER])
        at = table(step, [UNITS[u][1] for u in ORDER])
        unit = table(step, list(ORDER))
        head = 2 * lax.rem(x + hop, 4) + at
        q = qh[head]
        g = gh[head]
        levs = [lax.rem(level - k + LEVELS, LEVELS) for k in range(LEVELS)]
        key_row = lax.broadcasted_iota(jnp.int32, (TOK, ROWS), 0)
        query_tok = lax.rem(lax.broadcasted_iota(jnp.int32, (TOK, ROWS), 1), TOK)
        top = None
        for k in range(LEVELS):
            s = nt(kv[levs[k], head, 0], q) * SCORE_SCALE
            seen = key_row < lengths[k]
            if k == 0:
                seen = seen & (key_row <= query_tok)
            s = jnp.where(seen, s, -jnp.inf)
            score[k] = s
            high = jnp.max(s, axis=0, keepdims=True)
            top = high if top is None else jnp.maximum(top, high)
        total = None
        for k in range(LEVELS):
            e = jnp.exp2(score[k] - top)
            score[k] = e
            add = jnp.sum(e, axis=0, keepdims=True)
            total = add if total is None else total + add
        share = 1.0 / total
        out_t = None
        for k in range(LEVELS):
            w = score[k] * share
            score[k] = w
            low = w.astype(jnp.bfloat16)
            add = tn(kv[levs[k], head, 1], low)
            out_t = add if out_t is None else out_t + add
            dv = nn(low, g)
            if k % 2 == 0:
                part[unit, k // 2, 1] = dv
            else:
                sib_out[unit, k // 2, 1] = dv.astype(jnp.bfloat16)
        row_dot = jnp.sum(out_t * jnp.transpose(g.astype(jnp.float32)), axis=0, keepdims=True)
        dq_t = None
        for k in range(LEVELS):
            dw = nt(kv[levs[k], head, 1], g)
            ds = (score[k] * (dw - row_dot)).astype(jnp.bfloat16)
            add = tn(kv[levs[k], head, 0], ds)
            dq_t = add if dq_t is None else dq_t + add
            dk = nn(ds, q) * SCALE
            if k % 2 == 0:
                part[unit, k // 2, 0] = dk
            else:
                sib_out[unit, k // 2, 0] = dk.astype(jnp.bfloat16)
        out = jnp.transpose(out_t)
        dq = jnp.transpose(dq_t) * SCALE
        for r in range(2):
            wide_o[pl.ds(2 * head + r, TOK, stride=16), :] = out[r * TOK:(r + 1) * TOK]
            wide_q[pl.ds(2 * head + r, TOK, stride=16), :] = dq[r * TOK:(r + 1) * TOK]

    def add_sibling(unit):
        def first_even():
            wait_in(sib_in.at[unit, 0], sib_sem.at[unit, 0])
            part[unit, 0] = part[unit, 0] + sib_in[unit, 0].astype(jnp.float32)
        pl.when(even)(first_even)

        def first_last():
            wait_in(sib_in.at[unit, 0], sib_sem.at[unit, 0])
            part[unit, 1] = part[unit, 1] + sib_in[unit, 0].astype(jnp.float32)
        pl.when(level == 3)(first_last)

        def second():
            wait_in(sib_in.at[unit, 1], sib_sem.at[unit, 1])
            part[unit, 1] = part[unit, 1] + sib_in[unit, 1].astype(jnp.float32)
        pl.when(level == 2)(second)

    def finish(unit):
        add_sibling(unit)
        if unit in (0, 7):
            return
        for a in range(2):
            def body(a=a):
                got = part[unit, a]
                if unit in (5, 6):
                    wait_in(transit.at[a, unit - 5], transit_sem.at[a, unit - 5])
                    got = got + transit[a, unit - 5].astype(jnp.float32)
                x_out[a, unit - 1] = got.astype(jnp.bfloat16)
                start(("x", unit, a))
            when(cond_of[a], body)

    def gathered(a, at):
        for side in range(2):
            wait_in(x_in.at[a, at, side], x_sem.at[a, at, side])
        unit = 7 * at
        return (part[unit, a] + x_in[a, at, 0].astype(jnp.float32)
                + x_in[a, at, 1].astype(jnp.float32))

    def pass_down(at):
        def body():
            y_out[at] = gathered(1, at).astype(jnp.bfloat16)
            start(("down", at))
        pl.when(upper)(body)

    def before(unit):
        if unit == 0:
            arrive(1, 0)
            arrive(0, 1)
            arrive(0, 2)
        if unit == 1:
            arrive(1, 7)
            arrive(1, 2)
            arrive(1, 1)
        if unit == 2:
            arrive(0, 3)
            arrive(0, 4)
        if unit == 3:
            arrive(1, 3)
            arrive(0, 5)
        if unit == 4:
            arrive(1, 4)
            arrive(0, 6)
        if unit == 5:
            arrive(1, 5)
        if unit == 6:
            arrive(1, 6)
        from_sibling(unit)

    def after(unit):
        start(("part", unit, 0))
        start(("part", unit, 1))
        if unit > 0:
            finish(unit - 1)

    def step_body(step, carry):
        for at in range(8):
            pl.when(step == at)(functools.partial(before, ORDER[at]))
        compute(step)
        for at in range(8):
            pl.when(step == at)(functools.partial(after, ORDER[at]))
        return carry

    lax.fori_loop(0, 8, step_body, 0)
    pass_down(0)
    finish(7)
    pass_down(1)

    o_ref[...] = wide_o[...].astype(jnp.bfloat16)
    dq_ref[...] = wide_q[...].astype(jnp.bfloat16)

    for at in range(2):
        part[7 * at, 0] = gathered(0, at)

        def from_above(at=at):
            wait_in(y_in.at[at], y_sem.at[at])
            part[7 * at, 0] = part[7 * at, 0] + y_in[at].astype(jnp.float32)
        pl.when(level < 2)(from_above)
    for which, ref in ((0, dk_ref), (1, dv_ref)):
        for at in range(2):
            pair[pl.ds(at, TOK, stride=2), :] = part[7 * at, 0, which]
        ref[...] = pair[...].astype(jnp.bfloat16)

    for name, (cond, make, at) in sends.items():
        if name[0] == "sib" and name[1] == 1 or True:
            when(cond, lambda make=make, at=at: make(at).wait_send())


SENDS = 2 * (6 + 8) + 2 + 16 + 12 + 2


def shards(queries, keys, values, grad_out, parents, node_lengths):
    del parents
    tokens = queries.shape[0]
    wide_rows = tokens * KVH * 2
    vmem = pl.BlockSpec(memory_space=pltpu.VMEM)
    out = pl.pallas_call(
        kernel,
        out_shape=(
            jax.ShapeDtypeStruct((wide_rows, HD), jnp.bfloat16),
            jax.ShapeDtypeStruct((wide_rows, HD), jnp.bfloat16),
            jax.ShapeDtypeStruct((2 * tokens, HD), jnp.bfloat16),
            jax.ShapeDtypeStruct((2 * tokens, HD), jnp.bfloat16),
        ),
        in_specs=[vmem] * 4 + [pl.BlockSpec(memory_space=pltpu.SMEM)],
        out_specs=(vmem,) * 4,
        scratch_shapes=[
            pltpu.VMEM((LEVELS, KVH, 2, TOK, HD), jnp.bfloat16),
            pltpu.VMEM((KVH, ROWS, HD), jnp.bfloat16),
            pltpu.VMEM((KVH, ROWS, HD), jnp.bfloat16),
            pltpu.VMEM((wide_rows, HD), jnp.float32),
            pltpu.VMEM((wide_rows, HD), jnp.float32),
            pltpu.VMEM((2 * tokens, HD), jnp.float32),
            pltpu.VMEM((LEVELS, TOK, ROWS), jnp.float32),
            pltpu.VMEM((8, 2, 2, TOK, HD), jnp.float32),
            pltpu.VMEM((8, 2, 2, TOK, HD), jnp.bfloat16),
            pltpu.VMEM((8, 2, 2, TOK, HD), jnp.bfloat16),
            pltpu.VMEM((2, 6, 2, TOK, HD), jnp.bfloat16),
            pltpu.VMEM((2, 2, 2, 2, TOK, HD), jnp.bfloat16),
            pltpu.VMEM((2, 2, 2, TOK, HD), jnp.bfloat16),
            pltpu.VMEM((2, 2, TOK, HD), jnp.bfloat16),
            pltpu.VMEM((2, 2, TOK, HD), jnp.bfloat16),
            pltpu.SemaphoreType.DMA((LEVELS, 8)),
            pltpu.SemaphoreType.DMA((SENDS,)),
            pltpu.SemaphoreType.DMA((8, 2)),
            pltpu.SemaphoreType.DMA((2, 2, 2)),
            pltpu.SemaphoreType.DMA((2, 2)),
            pltpu.SemaphoreType.DMA((2,)),
        ],
        compiler_params=pltpu.CompilerParams(
            collective_id=0, has_side_effects=True, vmem_limit_bytes=48 * 1024 * 1024),
        cost_estimate=pl.CostEstimate(
            flops=12 * 16 * TOK * 4 * TOK * HD, bytes_accessed=5 * 1024 * 1024,
            transcendentals=16 * TOK * 4 * TOK),
    )(
        queries.reshape(wide_rows, HD),
        grad_out.reshape(wide_rows, HD),
        keys.reshape(2 * tokens, HD),
        values.reshape(2 * tokens, HD),
        node_lengths,
    )
    return (
        out[0].reshape(queries.shape),
        out[1].reshape(queries.shape),
        out[2].reshape(keys.shape),
        out[3].reshape(values.shape),
    )


def solution(mesh):
    in_specs = (
        P("node", None, "head", None),
        P("node", "head", None),
        P("node", "head", None),
        P("node", None, "head", None),
        P(),
        P(),
    )
    out_specs = (
        P("node", None, "head", None),
        P("node", None, "head", None),
        P("node", "head", None),
        P("node", "head", None),
    )
    return jax.shard_map(shards, mesh=mesh, in_specs=in_specs, out_specs=out_specs, check_vma=False)
```

```python
import functools
import math

import jax
import jax.numpy as jnp
from jax import lax
from jax.experimental import pallas as pl
from jax.experimental.pallas import tpu as pltpu
from jax.sharding import PartitionSpec as P

MESH = pl.DeviceIdType.MESH
VMEM_BYTES = 63 * 1024 * 1024
UNLOADS = 2
TOK = 256
LEVELS = 4
KVH = 8
HD = 128
ROWS = 512
SCALE = HD ** -0.5
SCORE_SCALE = SCALE * math.log2(math.e)

STEPS = ((0, 0), (1, 0), (2, 0), (3, 1), (2, 1), (3, 0), (1, 1), (0, 1))
VIA_X = (2, 4)


def nt(a, b):
    return lax.dot_general(a, b, (((1,), (1,)), ((), ())), preferred_element_type=jnp.float32)


def tn(a, b):
    return lax.dot_general(a, b, (((0,), (0,)), ((), ())), preferred_element_type=jnp.float32)


def nn(a, b):
    return lax.dot_general(a, b, (((1,), (0,)), ((), ())), preferred_element_type=jnp.float32)


def table(step, values):
    picked = jnp.int32(values[0])
    for at in range(1, len(values)):
        picked = jnp.where(step == at, jnp.int32(values[at]), picked)
    return picked


def kernel(
    q_hbm, g_hbm, k_hbm, v_hbm, len_hbm,
    o_hbm, dq_hbm, dk_hbm, dv_hbm,
    q_rows, g_rows, k_rows, v_rows, lens,
    kv, qh, gh, wide_o, wide_q, pair, score, low, ds, part,
    sib_out, sib_in, x_out, x_in, y_out, y_in, x_out_up, x_in_up,
    load_sem, store_sem, in_sem, out_sem, sib_sem, x_sem, x_up_sem, y_sem,
):
    loads = [
        pltpu.make_async_copy(src, dst, load_sem.at[at])
        for at, (src, dst) in enumerate((
            (k_hbm, k_rows), (v_hbm, v_rows), (q_hbm, q_rows), (g_hbm, g_rows), (len_hbm, lens)))
    ]
    for load in loads:
        load.start()
    p = lax.axis_index("node")
    x = lax.axis_index("head")
    level = lax.rem(p, LEVELS)
    odd = lax.rem(p, 2)
    upper = level >= 2
    lower = level < 2
    even = odd == 0
    up2 = jnp.maximum(level - 2, 0)
    y_node = p + 2 - 4 * (level // 2)
    to_sib = (p + 1 - 2 * odd, x)
    to_y = (y_node, x)

    def along(distance):
        return lax.rem(x + distance + 4, 4)

    def hop_of(step):
        return table(step, [hop for hop, _ in STEPS])

    def head_of(step):
        return 2 * along(hop_of(step)) + table(step, [at for _, at in STEPS])

    def remote(src, dst, kind, step, sem, device):
        return pltpu.make_async_remote_copy(
            src_ref=src, dst_ref=dst, send_sem=out_sem.at[kind, step], recv_sem=sem,
            device_id=device, device_id_type=MESH)

    def own_x(step):
        slot = kv.at[level, 2 * x + table(step, [at for _, at in STEPS])]
        return remote(slot, slot, 0, step, in_sem.at[level, step], (p, along(-hop_of(step))))

    def up_copy(step):
        slot = kv.at[level, head_of(step)]
        return remote(slot, slot, 1, step, in_sem.at[level, step], to_y)

    def pass_x(step):
        hop, at = STEPS[step]
        slot = kv.at[up2, 2 * x + at]
        return remote(slot, slot, 2, step, in_sem.at[up2, step], (p, along(-hop)))

    def to_sibling(a, step):
        lev = up2 if a else level
        slot = kv.at[lev, head_of(step)]
        return remote(slot, slot, 3 + a, step, in_sem.at[lev, step], to_sib)

    def part_copy(n, step):
        return remote(sib_out.at[step, n], sib_in.at[step, n], 5 + n, step,
                      sib_sem.at[step, n], to_sib)

    def x_copy(step):
        return remote(x_out.at[step], x_in.at[step], 7, step, x_sem.at[step],
                      (p, along(hop_of(step))))

    def x_up_copy(step):
        hop, at = STEPS[step]
        return remote(x_out_up.at[at], x_in_up.at[at], 8, step, x_up_sem.at[at], (p, along(hop)))

    def down_copy(step):
        return remote(y_out.at[step], y_in.at[step], 9, step, y_sem.at[step], to_y)

    def wait_in(dst, sem):
        pltpu.make_async_remote_copy(
            src_ref=dst, dst_ref=dst, send_sem=out_sem.at[0, 0], recv_sem=sem,
            device_id=to_sib, device_id_type=MESH).wait_recv()

    def wait_kv(lev, step):
        wait_in(kv.at[lev, head_of(step)], in_sem.at[lev, step])

    def from_sibling(step):
        pl.when(level >= 1)(lambda: wait_kv(jnp.maximum(level - 1, 0), step))
        pl.when(level == 3)(lambda: wait_kv(jnp.int32(0), step))

    barrier = pltpu.get_barrier_semaphore()
    friends = [to_sib, to_y] + [(p, along(hop)) for hop in (1, 2, 3)]
    for device in friends:
        pl.semaphore_signal(barrier, inc=1, device_id=device, device_id_type=MESH)

    for which, ref in ((0, k_rows), (1, v_rows)):
        loads[which].wait()
        pair[...] = ref[...].astype(jnp.float32)
        for at in range(2):
            kv[level, 2 * x + at, which] = pair[pl.ds(at, TOK, stride=2), :].astype(jnp.bfloat16)
    pl.semaphore_wait(barrier, len(friends))

    def first_lower():
        up_copy(0).start()
        up_copy(7).start()

    def first_even():
        to_sibling(0, 0).start()
        to_sibling(0, 7).start()

    pl.when(even)(first_even)
    pl.when(lower)(first_lower)
    for step in (1, 3, 5, 6):
        own_x(step).start()

    def blank():
        kv[3] = jnp.zeros((KVH, 2, TOK, HD), jnp.bfloat16)
    pl.when(level == 0)(blank)

    for at, (src, wide, dst) in enumerate(((q_rows, wide_o, qh), (g_rows, wide_q, gh))):
        loads[2 + at].wait()
        wide[...] = src[...].astype(jnp.float32)
        for head in range(KVH):
            for r in range(2):
                dst[head, r * TOK:(r + 1) * TOK, :] = (
                    wide[pl.ds(2 * head + r, TOK, stride=16), :].astype(jnp.bfloat16))

    loads[4].wait()
    lengths = []
    for k in range(LEVELS):
        real = lens[jnp.maximum(p - k, 0)]
        lengths.append(jnp.where(level >= k, real, 0))

    def compute(step, blocks):
        head = head_of(step)
        q = qh[head]
        g = gh[head]
        levs = [lax.rem(level - k + LEVELS, LEVELS) for k in range(blocks)]
        key_row = lax.broadcasted_iota(jnp.int32, (TOK, TOK), 0)
        query_tok = lax.broadcasted_iota(jnp.int32, (TOK, TOK), 1)
        floor = jnp.finfo(jnp.float32).min
        keys = jnp.concatenate([kv[lev, head, 0] for lev in levs], axis=0)
        vals = jnp.concatenate([kv[lev, head, 1] for lev in levs], axis=0)
        half_q = [q[r * TOK:(r + 1) * TOK] for r in range(2)]
        half_g = [g[r * TOK:(r + 1) * TOK] for r in range(2)]

        def block(got, k):
            return got[k * TOK:(k + 1) * TOK]

        def softmax(r, scores):
            tops, sums = [], []
            for k in range(blocks):
                seen = key_row < lengths[k]
                if k == 0:
                    seen = seen & (key_row <= query_tok)
                one = jnp.where(seen, block(scores, k) * SCORE_SCALE, -jnp.inf)
                high = jnp.maximum(jnp.max(one, axis=0, keepdims=True), floor)
                expo = jnp.exp2(one - high)
                score[r, k] = expo
                tops.append(high)
                sums.append(jnp.sum(expo, axis=0, keepdims=True))
            top = functools.reduce(jnp.maximum, tops)
            fades = [jnp.exp2(high - top) for high in tops]
            share = 1.0 / sum(one * fade for one, fade in zip(sums, fades))
            factors = [fade * share for fade in fades]
            for k in range(blocks):
                low[r, k] = (score[r, k] * factors[k]).astype(jnp.bfloat16)
            return factors

        def attend(r):
            weights = low[r, 0:blocks].reshape(blocks * TOK, TOK)
            return tn(vals, weights), nn(weights, half_g[r])

        def score_grads(r, out, dw, factors):
            turned = jnp.transpose(half_g[r].astype(jnp.float32))
            row_dot = jnp.sum(out * turned, axis=0, keepdims=True)
            for k in range(blocks):
                slope = (block(dw, k) - row_dot) * factors[k]
                ds[r, k] = (score[r, k] * slope).astype(jnp.bfloat16)

        def back(r):
            slopes = ds[r, 0:blocks].reshape(blocks * TOK, TOK)
            return tn(keys, slopes), nn(slopes, half_q[r])

        def give(r, out, dq):
            wide_o[pl.ds(2 * head + r, TOK, stride=16), :] = jnp.transpose(out)
            wide_q[pl.ds(2 * head + r, TOK, stride=16), :] = jnp.transpose(dq) * SCALE

        factors0 = softmax(0, nt(keys, half_q[0]))
        scores1 = nt(keys, half_q[1])
        out0, dv0 = attend(0)
        factors1 = softmax(1, scores1)
        dw0 = nt(vals, half_g[0])
        out1, dv1 = attend(1)
        score_grads(0, out0, dw0, factors0)
        dw1 = nt(vals, half_g[1])
        dq0, dk0 = back(0)
        score_grads(1, out1, dw1, factors1)
        dq1, dk1 = back(1)
        give(0, out0, dq0)
        give(1, out1, dq1)
        for k in range(blocks):
            for which, got in ((1, block(dv0, k) + block(dv1, k)),
                               (0, (block(dk0, k) + block(dk1, k)) * SCALE)):
                if k % 2 == 0:
                    part[step, k // 2, which] = got
                else:
                    sib_out[step, k // 2, which] = got.astype(jnp.bfloat16)

    def add_sibling(step):
        def add(a, n):
            wait_in(sib_in.at[step, n], sib_sem.at[step, n])
            part[step, a] = part[step, a] + sib_in[step, n].astype(jnp.float32)
        pl.when(even)(lambda: add(0, 0))
        pl.when(level == 3)(lambda: add(1, 0))
        pl.when(level == 2)(lambda: add(1, 1))

    def send_x(step):
        x_out[step] = part[step, 0].astype(jnp.bfloat16)
        x_copy(step).start()

    def finish_upper(step):
        add_sibling(step)
        pl.when((step > 0) & (step < 7))(lambda: send_x(step))
        direct = (step > 0) & (step < 7)
        for via in VIA_X:
            def along_x(via=via):
                x_out_up[STEPS[via][1]] = part[via, 1].astype(jnp.bfloat16)
                x_up_copy(via).start()
            pl.when(step == via)(along_x)
            direct = direct & (step != via)
        pl.when(direct)(lambda: send_down(step))

    def send_down(step):
        y_out[step] = part[step, 1].astype(jnp.bfloat16)
        down_copy(step).start()

    def pass_down(at):
        wait_in(x_in_up.at[at], x_up_sem.at[at])
        part[7 * at, 1] = part[7 * at, 1] + x_in_up[at].astype(jnp.float32)
        send_down(7 * at)

    def add_down(step):
        wait_in(y_in.at[step], y_sem.at[step])
        part[step, 0] = part[step, 0] + y_in[step].astype(jnp.float32)

    def take_down(step):
        direct = step > 0
        for via in VIA_X:
            direct = direct & (step != via)
        pl.when(direct)(lambda: add_down(step))
        send_x(step)

    def arrive_same(step):
        def body():
            wait_kv(level, step)
            pl.when(even)(lambda: to_sibling(0, step).start())
        pl.when((step > 0) & (step < 7))(body)

    def arrive_upper(step):
        def below():
            wait_kv(up2, step)
            to_sibling(1, step).start()

        def last_early():
            wait_kv(up2, 7)
            pass_x(VIA_X[1]).start()
            to_sibling(1, 7).start()

        pl.when(step < 7)(below)
        pl.when(step == 0)(lambda: pass_x(VIA_X[0]).start())
        pl.when(step == 1)(last_early)
        arrive_same(step)

    def step_upper(step):
        pl.when(step < 2)(lambda: own_x(2 * step + 2).start())
        pl.when(step == 0)(lambda: arrive_upper(step))
        pl.when((step > 1) & (step < 7))(lambda: arrive_upper(step))
        pl.when(step > 0)(lambda: finish_upper(step - 1))
        pl.when(step == 6)(lambda: pass_down(0))
        from_sibling(step)
        pl.when(level == 3)(lambda: compute(step, 4))
        pl.when(level == 2)(lambda: compute(step, 3))
        part_copy(0, step).start()
        pl.when(level == 3)(lambda: part_copy(1, step).start())
        pl.when(step == 0)(lambda: arrive_upper(step + 1))

    def step_lower(step):
        pl.when(step < 2)(lambda: own_x(2 * step + 2).start())
        arrive_same(step)
        pl.when((step > 0) & (step < 7) & (step != VIA_X[0]) & (step != VIA_X[1]))(
            lambda: up_copy(step).start())
        pl.when((step > 0) & even)(lambda: add_sibling(step - 1))
        from_sibling(step)
        compute(step, 2)
        pl.when(level == 1)(lambda: part_copy(0, step).start())

    def step_body(step, carry):
        pl.when(upper)(lambda: step_upper(step))
        pl.when(lower)(lambda: step_lower(step))
        return carry

    lax.fori_loop(0, 8, step_body, 0)

    def last_upper():
        finish_upper(jnp.int32(7))
        pass_down(1)

    def last_lower():
        pl.when(even)(lambda: add_sibling(jnp.int32(7)))

        def down_body(step, carry):
            take_down(step)
            return carry
        lax.fori_loop(1, 7, down_body, 0)

    pl.when(upper)(last_upper)
    q_rows[...] = wide_o[...].astype(jnp.bfloat16)
    g_rows[...] = wide_q[...].astype(jnp.bfloat16)
    stores = [
        pltpu.make_async_copy(src, dst, store_sem.at[at])
        for at, (src, dst) in enumerate((
            (q_rows, o_hbm), (g_rows, dq_hbm), (k_rows, dk_hbm), (v_rows, dv_hbm)))
    ]
    stores[0].start()
    stores[1].start()
    pl.when(lower)(last_lower)

    for at in range(2):
        mine = 7 * at
        for step in range(1, 7):
            if STEPS[step][1] == at:
                wait_in(x_in.at[step], x_sem.at[step])
                part[mine, 0] = part[mine, 0] + x_in[step].astype(jnp.float32)
        pl.when(lower)(functools.partial(add_down, mine))
    for which, ref in ((0, k_rows), (1, v_rows)):
        for at in range(2):
            pair[pl.ds(at, TOK, stride=2), :] = part[7 * at, 0, which]
        ref[...] = pair[...].astype(jnp.bfloat16)
        stores[2 + which].start()

    for step in range(8):
        if 0 < step < 7:
            own_x(step).wait_send()
            x_copy(step).wait_send()
        if step in VIA_X:
            pl.when(upper)(lambda step=step: pass_x(step).wait_send())
            pl.when(upper)(lambda step=step: x_up_copy(step).wait_send())
        else:
            pl.when(lower)(lambda step=step: up_copy(step).wait_send())
            pl.when(upper)(lambda step=step: down_copy(step).wait_send())
        pl.when(even)(lambda step=step: to_sibling(0, step).wait_send())
        pl.when(upper)(lambda step=step: to_sibling(1, step).wait_send())
        pl.when(level >= 1)(lambda step=step: part_copy(0, step).wait_send())
        pl.when(level == 3)(lambda step=step: part_copy(1, step).wait_send())
    for store in stores:
        store.wait()


def unload(*refs):
    held, load_sem, store_sem = refs[8:12], refs[12], refs[13]
    moves = []
    for at in range(4):
        rows = refs[at].shape[0] // UNLOADS
        for piece in range(UNLOADS):
            cut = pl.ds(piece * rows, rows)
            moves.append((
                pltpu.make_async_copy(refs[at].at[cut], held[at].at[cut], load_sem.at[at, piece]),
                pltpu.make_async_copy(held[at].at[cut], refs[4 + at].at[cut], store_sem.at[at, piece])))
    for load, _ in moves:
        load.start()
    for load, store in moves:
        load.wait()
        store.start()
    for _, store in moves:
        store.wait()


def shards(queries, keys, values, grad_out, parents, node_lengths):
    del parents
    tokens = queries.shape[0]
    wide_rows = tokens * KVH * 2
    hbm = pl.BlockSpec(memory_space=pltpu.HBM)
    out = pl.pallas_call(
        kernel,
        out_shape=(
            jax.ShapeDtypeStruct((wide_rows, HD), jnp.bfloat16),
            jax.ShapeDtypeStruct((wide_rows, HD), jnp.bfloat16),
            jax.ShapeDtypeStruct((2 * tokens, HD), jnp.bfloat16),
            jax.ShapeDtypeStruct((2 * tokens, HD), jnp.bfloat16),
        ),
        in_specs=[hbm] * 5,
        out_specs=(hbm,) * 4,
        scratch_shapes=[
            pltpu.VMEM((wide_rows, HD), jnp.bfloat16),
            pltpu.VMEM((wide_rows, HD), jnp.bfloat16),
            pltpu.VMEM((2 * tokens, HD), jnp.bfloat16),
            pltpu.VMEM((2 * tokens, HD), jnp.bfloat16),
            pltpu.SMEM(node_lengths.shape, jnp.int32),
            pltpu.VMEM((LEVELS, KVH, 2, TOK, HD), jnp.bfloat16),
            pltpu.VMEM((KVH, ROWS, HD), jnp.bfloat16),
            pltpu.VMEM((KVH, ROWS, HD), jnp.bfloat16),
            pltpu.VMEM((wide_rows, HD), jnp.float32),
            pltpu.VMEM((wide_rows, HD), jnp.float32),
            pltpu.VMEM((2 * tokens, HD), jnp.float32),
            pltpu.VMEM((2, LEVELS, TOK, TOK), jnp.float32),
            pltpu.VMEM((2, LEVELS, TOK, TOK), jnp.bfloat16),
            pltpu.VMEM((2, LEVELS, TOK, TOK), jnp.bfloat16),
            pltpu.VMEM((8, 2, 2, TOK, HD), jnp.float32),
            pltpu.VMEM((8, 2, 2, TOK, HD), jnp.bfloat16),
            pltpu.VMEM((8, 2, 2, TOK, HD), jnp.bfloat16),
            pltpu.VMEM((8, 2, TOK, HD), jnp.bfloat16),
            pltpu.VMEM((8, 2, TOK, HD), jnp.bfloat16),
            pltpu.VMEM((8, 2, TOK, HD), jnp.bfloat16),
            pltpu.VMEM((8, 2, TOK, HD), jnp.bfloat16),
            pltpu.VMEM((2, 2, TOK, HD), jnp.bfloat16),
            pltpu.VMEM((2, 2, TOK, HD), jnp.bfloat16),
            pltpu.SemaphoreType.DMA((5,)),
            pltpu.SemaphoreType.DMA((4,)),
            pltpu.SemaphoreType.DMA((LEVELS, 8)),
            pltpu.SemaphoreType.DMA((10, 8)),
            pltpu.SemaphoreType.DMA((8, 2)),
            pltpu.SemaphoreType.DMA((8,)),
            pltpu.SemaphoreType.DMA((2,)),
            pltpu.SemaphoreType.DMA((8,)),
        ],
        compiler_params=pltpu.CompilerParams(
            collective_id=0, has_side_effects=True, vmem_limit_bytes=VMEM_BYTES),
        cost_estimate=pl.CostEstimate(
            flops=12 * 16 * TOK * 4 * TOK * HD, bytes_accessed=5 * 1024 * 1024,
            transcendentals=16 * TOK * 4 * TOK),
    )(
        queries.reshape(wide_rows, HD),
        grad_out.reshape(wide_rows, HD),
        keys.reshape(2 * tokens, HD),
        values.reshape(2 * tokens, HD),
        node_lengths,
    )
    out = pl.pallas_call(
        unload,
        out_shape=tuple(jax.ShapeDtypeStruct(one.shape, one.dtype) for one in out),
        in_specs=[hbm] * 4,
        out_specs=(hbm,) * 4,
        scratch_shapes=[pltpu.VMEM(one.shape, one.dtype) for one in out]
        + [pltpu.SemaphoreType.DMA((4, UNLOADS))] * 2,
        compiler_params=pltpu.CompilerParams(vmem_limit_bytes=VMEM_BYTES),
    )(*out)
    return (
        out[0].reshape(queries.shape),
        out[1].reshape(queries.shape),
        out[2].reshape(keys.shape),
        out[3].reshape(values.shape),
    )


def solution(mesh):
    in_specs = (
        P("node", None, "head", None),
        P("node", "head", None),
        P("node", "head", None),
        P("node", None, "head", None),
        P(),
        P(),
    )
    out_specs = (
        P("node", None, "head", None),
        P("node", None, "head", None),
        P("node", "head", None),
        P("node", "head", None),
    )
    return jax.shard_map(shards, mesh=mesh, in_specs=in_specs, out_specs=out_specs, check_vma=False)
```

```python
import functools
import math

import jax
import jax.numpy as jnp
from jax import lax
from jax.experimental import pallas as pl
from jax.experimental.pallas import tpu as pltpu
from jax.sharding import PartitionSpec as P

MESH = pl.DeviceIdType.MESH
VMEM_BYTES = 63 * 1024 * 1024
UNLOADS = 2
TOK = 256
LEVELS = 4
KVH = 8
HD = 128
ROWS = 512
SCALE = HD ** -0.5
SCORE_SCALE = SCALE * math.log2(math.e)

STEPS = ((0, 0), (1, 0), (3, 0), (3, 1), (1, 1), (2, 0), (2, 1), (0, 1))
VIA_X = (2, 4)


def nt(a, b):
    return lax.dot_general(a, b, (((1,), (1,)), ((), ())), preferred_element_type=jnp.float32)


def tn(a, b):
    return lax.dot_general(a, b, (((0,), (0,)), ((), ())), preferred_element_type=jnp.float32)


def nn(a, b):
    return lax.dot_general(a, b, (((1,), (0,)), ((), ())), preferred_element_type=jnp.float32)


def table(step, values):
    picked = jnp.int32(values[0])
    for at in range(1, len(values)):
        picked = jnp.where(step == at, jnp.int32(values[at]), picked)
    return picked


def kernel(
    q_hbm, g_hbm, k_hbm, v_hbm, len_hbm,
    o_hbm, dq_hbm, dk_hbm, dv_hbm,
    q_rows, g_rows, k_rows, v_rows, lens,
    kv, qh, gh, wide_o, wide_q, pair, score, low, ds, part,
    sib_out, sib_in, x_out, x_in, y_out, y_in, x_out_up, x_in_up,
    load_sem, store_sem, in_sem, out_sem, sib_sem, x_sem, x_up_sem, y_sem,
):
    loads = [
        pltpu.make_async_copy(src, dst, load_sem.at[at])
        for at, (src, dst) in enumerate((
            (k_hbm, k_rows), (v_hbm, v_rows), (q_hbm, q_rows), (g_hbm, g_rows), (len_hbm, lens)))
    ]
    for load in loads:
        load.start()
    p = lax.axis_index("node")
    x = lax.axis_index("head")
    level = lax.rem(p, LEVELS)
    odd = lax.rem(p, 2)
    upper = level >= 2
    lower = level < 2
    even = odd == 0
    up2 = jnp.maximum(level - 2, 0)
    y_node = p + 2 - 4 * (level // 2)
    to_sib = (p + 1 - 2 * odd, x)
    to_y = (y_node, x)

    def along(distance):
        return lax.rem(x + distance + 4, 4)

    def hop_of(step):
        return table(step, [hop for hop, _ in STEPS])

    def head_of(step):
        return 2 * along(hop_of(step)) + table(step, [at for _, at in STEPS])

    def remote(src, dst, kind, step, sem, device):
        return pltpu.make_async_remote_copy(
            src_ref=src, dst_ref=dst, send_sem=out_sem.at[kind, step], recv_sem=sem,
            device_id=device, device_id_type=MESH)

    def own_x(step):
        slot = kv.at[level, 2 * x + table(step, [at for _, at in STEPS])]
        return remote(slot, slot, 0, step, in_sem.at[level, step], (p, along(-hop_of(step))))

    def up_copy(step):
        slot = kv.at[level, head_of(step)]
        return remote(slot, slot, 1, step, in_sem.at[level, step], to_y)

    def pass_x(step):
        hop, at = STEPS[step]
        slot = kv.at[up2, 2 * x + at]
        return remote(slot, slot, 2, step, in_sem.at[up2, step], (p, along(-hop)))

    def to_sibling(a, step):
        lev = up2 if a else level
        slot = kv.at[lev, head_of(step)]
        return remote(slot, slot, 3 + a, step, in_sem.at[lev, step], to_sib)

    def part_copy(n, step):
        return remote(sib_out.at[step, n], sib_in.at[step, n], 5 + n, step,
                      sib_sem.at[step, n], to_sib)

    def x_copy(step):
        return remote(x_out.at[step], x_in.at[step], 7, step, x_sem.at[step],
                      (p, along(hop_of(step))))

    def x_up_copy(step):
        hop, at = STEPS[step]
        return remote(x_out_up.at[at], x_in_up.at[at], 8, step, x_up_sem.at[at], (p, along(hop)))

    def down_copy(step):
        return remote(y_out.at[step], y_in.at[step], 9, step, y_sem.at[step], to_y)

    def wait_in(dst, sem):
        pltpu.make_async_remote_copy(
            src_ref=dst, dst_ref=dst, send_sem=out_sem.at[0, 0], recv_sem=sem,
            device_id=to_sib, device_id_type=MESH).wait_recv()

    def wait_kv(lev, step):
        wait_in(kv.at[lev, head_of(step)], in_sem.at[lev, step])

    def from_sibling(step):
        pl.when(level >= 1)(lambda: wait_kv(jnp.maximum(level - 1, 0), step))
        pl.when(level == 3)(lambda: wait_kv(jnp.int32(0), step))

    barrier = pltpu.get_barrier_semaphore()
    friends = [to_sib, to_y] + [(p, along(hop)) for hop in (1, 2, 3)]
    for device in friends:
        pl.semaphore_signal(barrier, inc=1, device_id=device, device_id_type=MESH)

    for which, ref in ((0, k_rows), (1, v_rows)):
        loads[which].wait()
        pair[...] = ref[...].astype(jnp.float32)
        for at in range(2):
            kv[level, 2 * x + at, which] = pair[pl.ds(at, TOK, stride=2), :].astype(jnp.bfloat16)
    pl.semaphore_wait(barrier, len(friends))

    def first_lower():
        up_copy(0).start()
        up_copy(7).start()

    def first_even():
        to_sibling(0, 0).start()
        to_sibling(0, 7).start()

    pl.when(even)(first_even)
    pl.when(lower)(first_lower)
    for step in (1, 3, 2, 4):
        own_x(step).start()

    def blank():
        kv[3] = jnp.zeros((KVH, 2, TOK, HD), jnp.bfloat16)
    pl.when(level == 0)(blank)

    for at, (src, wide, dst) in enumerate(((q_rows, wide_o, qh), (g_rows, wide_q, gh))):
        loads[2 + at].wait()
        wide[...] = src[...].astype(jnp.float32)
        for head in range(KVH):
            for r in range(2):
                dst[head, r * TOK:(r + 1) * TOK, :] = (
                    wide[pl.ds(2 * head + r, TOK, stride=16), :].astype(jnp.bfloat16))

    loads[4].wait()
    lengths = []
    for k in range(LEVELS):
        real = lens[jnp.maximum(p - k, 0)]
        lengths.append(jnp.where(level >= k, real, 0))

    def compute(step, blocks):
        head = head_of(step)
        q = qh[head]
        g = gh[head]
        levs = [lax.rem(level - k + LEVELS, LEVELS) for k in range(blocks)]
        key_row = lax.broadcasted_iota(jnp.int32, (TOK, TOK), 0)
        query_tok = lax.broadcasted_iota(jnp.int32, (TOK, TOK), 1)
        floor = jnp.finfo(jnp.float32).min
        keys = jnp.concatenate([kv[lev, head, 0] for lev in levs], axis=0)
        vals = jnp.concatenate([kv[lev, head, 1] for lev in levs], axis=0)
        half_q = [q[r * TOK:(r + 1) * TOK] for r in range(2)]
        half_g = [g[r * TOK:(r + 1) * TOK] for r in range(2)]

        def block(got, k):
            return got[k * TOK:(k + 1) * TOK]

        def softmax(r, scores):
            tops, sums = [], []
            for k in range(blocks):
                seen = key_row < lengths[k]
                if k == 0:
                    seen = seen & (key_row <= query_tok)
                one = jnp.where(seen, block(scores, k) * SCORE_SCALE, -jnp.inf)
                high = jnp.maximum(jnp.max(one, axis=0, keepdims=True), floor)
                expo = jnp.exp2(one - high)
                score[r, k] = expo
                tops.append(high)
                sums.append(jnp.sum(expo, axis=0, keepdims=True))
            top = functools.reduce(jnp.maximum, tops)
            fades = [jnp.exp2(high - top) for high in tops]
            share = 1.0 / sum(one * fade for one, fade in zip(sums, fades))
            factors = [fade * share for fade in fades]
            for k in range(blocks):
                low[r, k] = (score[r, k] * factors[k]).astype(jnp.bfloat16)
            return factors

        def attend(r):
            weights = low[r, 0:blocks].reshape(blocks * TOK, TOK)
            return tn(vals, weights), nn(weights, half_g[r])

        def score_grads(r, out, dw, factors):
            turned = jnp.transpose(half_g[r].astype(jnp.float32))
            row_dot = jnp.sum(out * turned, axis=0, keepdims=True)
            for k in range(blocks):
                slope = (block(dw, k) - row_dot) * factors[k]
                ds[r, k] = (score[r, k] * slope).astype(jnp.bfloat16)

        def back(r):
            slopes = ds[r, 0:blocks].reshape(blocks * TOK, TOK)
            return tn(keys, slopes), nn(slopes, half_q[r])

        def give(r, out, dq):
            wide_o[pl.ds(2 * head + r, TOK, stride=16), :] = jnp.transpose(out)
            wide_q[pl.ds(2 * head + r, TOK, stride=16), :] = jnp.transpose(dq) * SCALE

        factors0 = softmax(0, nt(keys, half_q[0]))
        scores1 = nt(keys, half_q[1])
        out0, dv0 = attend(0)
        factors1 = softmax(1, scores1)
        dw0 = nt(vals, half_g[0])
        out1, dv1 = attend(1)
        score_grads(0, out0, dw0, factors0)
        dw1 = nt(vals, half_g[1])
        dq0, dk0 = back(0)
        score_grads(1, out1, dw1, factors1)
        dq1, dk1 = back(1)
        give(0, out0, dq0)
        give(1, out1, dq1)
        for k in range(blocks):
            for which, got in ((1, block(dv0, k) + block(dv1, k)),
                               (0, (block(dk0, k) + block(dk1, k)) * SCALE)):
                if k % 2 == 0:
                    part[step, k // 2, which] = got
                else:
                    sib_out[step, k // 2, which] = got.astype(jnp.bfloat16)

    def add_sibling(step):
        def add(a, n):
            wait_in(sib_in.at[step, n], sib_sem.at[step, n])
            part[step, a] = part[step, a] + sib_in[step, n].astype(jnp.float32)
        pl.when(even)(lambda: add(0, 0))
        pl.when(level == 3)(lambda: add(1, 0))
        pl.when(level == 2)(lambda: add(1, 1))

    def send_x(step):
        x_out[step] = part[step, 0].astype(jnp.bfloat16)
        x_copy(step).start()

    def finish_upper(step):
        add_sibling(step)
        pl.when((step > 0) & (step < 7))(lambda: send_x(step))
        direct = (step > 0) & (step < 7)
        for via in VIA_X:
            def along_x(via=via):
                x_out_up[STEPS[via][1]] = part[via, 1].astype(jnp.bfloat16)
                x_up_copy(via).start()
            pl.when(step == via)(along_x)
            direct = direct & (step != via)
        pl.when(direct)(lambda: send_down(step))

    def send_down(step):
        y_out[step] = part[step, 1].astype(jnp.bfloat16)
        down_copy(step).start()

    def pass_down(at):
        wait_in(x_in_up.at[at], x_up_sem.at[at])
        part[7 * at, 1] = part[7 * at, 1] + x_in_up[at].astype(jnp.float32)
        send_down(7 * at)

    def add_down(step):
        wait_in(y_in.at[step], y_sem.at[step])
        part[step, 0] = part[step, 0] + y_in[step].astype(jnp.float32)

    def take_down(step):
        direct = step > 0
        for via in VIA_X:
            direct = direct & (step != via)
        pl.when(direct)(lambda: add_down(step))
        send_x(step)

    def arrive_same(step):
        def body():
            wait_kv(level, step)
            pl.when(even)(lambda: to_sibling(0, step).start())
        pl.when((step > 0) & (step < 7))(body)

    def arrive_upper(step):
        def below():
            wait_kv(up2, step)
            to_sibling(1, step).start()

        def last_early():
            wait_kv(up2, 7)
            pass_x(VIA_X[1]).start()
            to_sibling(1, 7).start()

        pl.when(step < 7)(below)
        pl.when(step == 0)(lambda: pass_x(VIA_X[0]).start())
        pl.when(step == 1)(last_early)
        arrive_same(step)

    def step_upper(step):
        pl.when(step < 2)(lambda: own_x(step + 5).start())
        pl.when(step == 0)(lambda: arrive_upper(step))
        pl.when(step == 2)(lambda: arrive_upper(step))
        pl.when((step > 1) & (step < 6))(lambda: arrive_upper(step + 1))
        pl.when(step > 0)(lambda: finish_upper(step - 1))
        pl.when(step == 6)(lambda: pass_down(0))
        from_sibling(step)
        pl.when(level == 3)(lambda: compute(step, 4))
        pl.when(level == 2)(lambda: compute(step, 3))
        part_copy(0, step).start()
        pl.when(level == 3)(lambda: part_copy(1, step).start())
        pl.when(step == 0)(lambda: arrive_upper(step + 1))

    def step_lower(step):
        pl.when(step < 2)(lambda: own_x(step + 5).start())
        arrive_same(step)
        pl.when((step > 0) & (step < 7) & (step != VIA_X[0]) & (step != VIA_X[1]))(
            lambda: up_copy(step).start())
        pl.when((step > 0) & even)(lambda: add_sibling(step - 1))
        from_sibling(step)
        compute(step, 2)
        pl.when(level == 1)(lambda: part_copy(0, step).start())

    def step_body(step, carry):
        pl.when(upper)(lambda: step_upper(step))
        pl.when(lower)(lambda: step_lower(step))
        return carry

    lax.fori_loop(0, 8, step_body, 0)

    def last_upper():
        finish_upper(jnp.int32(7))
        pass_down(1)

    def last_lower():
        pl.when(even)(lambda: add_sibling(jnp.int32(7)))

        def down_body(step, carry):
            take_down(step)
            return carry
        lax.fori_loop(1, 7, down_body, 0)

    pl.when(upper)(last_upper)
    q_rows[...] = wide_o[...].astype(jnp.bfloat16)
    g_rows[...] = wide_q[...].astype(jnp.bfloat16)
    stores = [
        pltpu.make_async_copy(src, dst, store_sem.at[at])
        for at, (src, dst) in enumerate((
            (q_rows, o_hbm), (g_rows, dq_hbm), (k_rows, dk_hbm), (v_rows, dv_hbm)))
    ]
    stores[0].start()
    stores[1].start()
    pl.when(lower)(last_lower)

    for at in range(2):
        mine = 7 * at
        for step in range(1, 7):
            if STEPS[step][1] == at:
                wait_in(x_in.at[step], x_sem.at[step])
                part[mine, 0] = part[mine, 0] + x_in[step].astype(jnp.float32)
        pl.when(lower)(functools.partial(add_down, mine))
    for which, ref in ((0, k_rows), (1, v_rows)):
        for at in range(2):
            pair[pl.ds(at, TOK, stride=2), :] = part[7 * at, 0, which]
        ref[...] = pair[...].astype(jnp.bfloat16)
        stores[2 + which].start()

    for step in range(8):
        if 0 < step < 7:
            own_x(step).wait_send()
            x_copy(step).wait_send()
        if step in VIA_X:
            pl.when(upper)(lambda step=step: pass_x(step).wait_send())
            pl.when(upper)(lambda step=step: x_up_copy(step).wait_send())
        else:
            pl.when(lower)(lambda step=step: up_copy(step).wait_send())
            pl.when(upper)(lambda step=step: down_copy(step).wait_send())
        pl.when(even)(lambda step=step: to_sibling(0, step).wait_send())
        pl.when(upper)(lambda step=step: to_sibling(1, step).wait_send())
        pl.when(level >= 1)(lambda step=step: part_copy(0, step).wait_send())
        pl.when(level == 3)(lambda step=step: part_copy(1, step).wait_send())
    for store in stores:
        store.wait()


def unload(*refs):
    held, load_sem, store_sem = refs[8:12], refs[12], refs[13]
    moves = []
    for at in range(4):
        rows = refs[at].shape[0] // UNLOADS
        for piece in range(UNLOADS):
            cut = pl.ds(piece * rows, rows)
            moves.append((
                pltpu.make_async_copy(refs[at].at[cut], held[at].at[cut], load_sem.at[at, piece]),
                pltpu.make_async_copy(held[at].at[cut], refs[4 + at].at[cut], store_sem.at[at, piece])))
    for load, _ in moves:
        load.start()
    for load, store in moves:
        load.wait()
        store.start()
    for _, store in moves:
        store.wait()


def shards(queries, keys, values, grad_out, parents, node_lengths):
    del parents
    tokens = queries.shape[0]
    wide_rows = tokens * KVH * 2
    hbm = pl.BlockSpec(memory_space=pltpu.HBM)
    out = pl.pallas_call(
        kernel,
        out_shape=(
            jax.ShapeDtypeStruct((wide_rows, HD), jnp.bfloat16),
            jax.ShapeDtypeStruct((wide_rows, HD), jnp.bfloat16),
            jax.ShapeDtypeStruct((2 * tokens, HD), jnp.bfloat16),
            jax.ShapeDtypeStruct((2 * tokens, HD), jnp.bfloat16),
        ),
        in_specs=[hbm] * 5,
        out_specs=(hbm,) * 4,
        scratch_shapes=[
            pltpu.VMEM((wide_rows, HD), jnp.bfloat16),
            pltpu.VMEM((wide_rows, HD), jnp.bfloat16),
            pltpu.VMEM((2 * tokens, HD), jnp.bfloat16),
            pltpu.VMEM((2 * tokens, HD), jnp.bfloat16),
            pltpu.SMEM(node_lengths.shape, jnp.int32),
            pltpu.VMEM((LEVELS, KVH, 2, TOK, HD), jnp.bfloat16),
            pltpu.VMEM((KVH, ROWS, HD), jnp.bfloat16),
            pltpu.VMEM((KVH, ROWS, HD), jnp.bfloat16),
            pltpu.VMEM((wide_rows, HD), jnp.float32),
            pltpu.VMEM((wide_rows, HD), jnp.float32),
            pltpu.VMEM((2 * tokens, HD), jnp.float32),
            pltpu.VMEM((2, LEVELS, TOK, TOK), jnp.float32),
            pltpu.VMEM((2, LEVELS, TOK, TOK), jnp.bfloat16),
            pltpu.VMEM((2, LEVELS, TOK, TOK), jnp.bfloat16),
            pltpu.VMEM((8, 2, 2, TOK, HD), jnp.float32),
            pltpu.VMEM((8, 2, 2, TOK, HD), jnp.bfloat16),
            pltpu.VMEM((8, 2, 2, TOK, HD), jnp.bfloat16),
            pltpu.VMEM((8, 2, TOK, HD), jnp.bfloat16),
            pltpu.VMEM((8, 2, TOK, HD), jnp.bfloat16),
            pltpu.VMEM((8, 2, TOK, HD), jnp.bfloat16),
            pltpu.VMEM((8, 2, TOK, HD), jnp.bfloat16),
            pltpu.VMEM((2, 2, TOK, HD), jnp.bfloat16),
            pltpu.VMEM((2, 2, TOK, HD), jnp.bfloat16),
            pltpu.SemaphoreType.DMA((5,)),
            pltpu.SemaphoreType.DMA((4,)),
            pltpu.SemaphoreType.DMA((LEVELS, 8)),
            pltpu.SemaphoreType.DMA((10, 8)),
            pltpu.SemaphoreType.DMA((8, 2)),
            pltpu.SemaphoreType.DMA((8,)),
            pltpu.SemaphoreType.DMA((2,)),
            pltpu.SemaphoreType.DMA((8,)),
        ],
        compiler_params=pltpu.CompilerParams(
            collective_id=0, has_side_effects=True, vmem_limit_bytes=VMEM_BYTES),
        cost_estimate=pl.CostEstimate(
            flops=12 * 16 * TOK * 4 * TOK * HD, bytes_accessed=5 * 1024 * 1024,
            transcendentals=16 * TOK * 4 * TOK),
    )(
        queries.reshape(wide_rows, HD),
        grad_out.reshape(wide_rows, HD),
        keys.reshape(2 * tokens, HD),
        values.reshape(2 * tokens, HD),
        node_lengths,
    )
    out = pl.pallas_call(
        unload,
        out_shape=tuple(jax.ShapeDtypeStruct(one.shape, one.dtype) for one in out),
        in_specs=[hbm] * 4,
        out_specs=(hbm,) * 4,
        scratch_shapes=[pltpu.VMEM(one.shape, one.dtype) for one in out]
        + [pltpu.SemaphoreType.DMA((4, UNLOADS))] * 2,
        compiler_params=pltpu.CompilerParams(vmem_limit_bytes=VMEM_BYTES),
    )(*out)
    return (
        out[0].reshape(queries.shape),
        out[1].reshape(queries.shape),
        out[2].reshape(keys.shape),
        out[3].reshape(values.shape),
    )


def solution(mesh):
    in_specs = (
        P("node", None, "head", None),
        P("node", "head", None),
        P("node", "head", None),
        P("node", None, "head", None),
        P(),
        P(),
    )
    out_specs = (
        P("node", None, "head", None),
        P("node", None, "head", None),
        P("node", "head", None),
        P("node", "head", None),
    )
    return jax.shard_map(shards, mesh=mesh, in_specs=in_specs, out_specs=out_specs, check_vma=False)
```

```python
import functools
import math

import jax
import jax.numpy as jnp
from jax import lax
from jax.experimental import pallas as pl
from jax.experimental.pallas import tpu as pltpu
from jax.sharding import PartitionSpec as P

MESH = pl.DeviceIdType.MESH
VMEM_BYTES = 63 * 1024 * 1024
UNLOADS = 2
TOK = 256
LEVELS = 4
KVH = 8
HD = 128
ROWS = 512
SCALE = HD ** -0.5
SCORE_SCALE = SCALE * math.log2(math.e)

STEPS = ((0, 0), (1, 0), (3, 0), (3, 1), (1, 1), (2, 0), (2, 1), (0, 1))
VIA_X = (2, 4)


def nt(a, b):
    return lax.dot_general(a, b, (((1,), (1,)), ((), ())), preferred_element_type=jnp.float32)


def tn(a, b):
    return lax.dot_general(a, b, (((0,), (0,)), ((), ())), preferred_element_type=jnp.float32)


def nn(a, b):
    return lax.dot_general(a, b, (((1,), (0,)), ((), ())), preferred_element_type=jnp.float32)


def table(step, values):
    picked = jnp.int32(values[0])
    for at in range(1, len(values)):
        picked = jnp.where(step == at, jnp.int32(values[at]), picked)
    return picked


def kernel(
    q_hbm, g_hbm, k_hbm, v_hbm, len_hbm,
    o_hbm, dq_hbm, dk_hbm, dv_hbm,
    q_rows, g_rows, k_rows, v_rows, lens,
    kv, qh, gh, wide_o, wide_q, pair, score, low, ds, part,
    sib_out, sib_in, x_out, x_in, y_out, y_in, x_out_up, x_in_up,
    load_sem, store_sem, half_sem, in_sem, out_sem, sib_sem, x_sem, x_up_sem, y_sem,
):
    loads = [
        pltpu.make_async_copy(src, dst, load_sem.at[at])
        for at, (src, dst) in enumerate((
            (k_hbm, k_rows), (v_hbm, v_rows), (q_hbm, q_rows), (g_hbm, g_rows), (len_hbm, lens)))
    ]
    for load in loads:
        load.start()
    p = lax.axis_index("node")
    x = lax.axis_index("head")
    level = lax.rem(p, LEVELS)
    odd = lax.rem(p, 2)
    upper = level >= 2
    lower = level < 2
    even = odd == 0
    up2 = jnp.maximum(level - 2, 0)
    y_node = p + 2 - 4 * (level // 2)
    to_sib = (p + 1 - 2 * odd, x)
    to_y = (y_node, x)

    def along(distance):
        return lax.rem(x + distance + 4, 4)

    def hop_of(step):
        return table(step, [hop for hop, _ in STEPS])

    def head_of(step):
        return 2 * along(hop_of(step)) + table(step, [at for _, at in STEPS])

    def remote(src, dst, kind, step, sem, device):
        return pltpu.make_async_remote_copy(
            src_ref=src, dst_ref=dst, send_sem=out_sem.at[kind, step], recv_sem=sem,
            device_id=device, device_id_type=MESH)

    def own_x(step):
        slot = kv.at[level, 2 * x + table(step, [at for _, at in STEPS])]
        return remote(slot, slot, 0, step, in_sem.at[level, step], (p, along(-hop_of(step))))

    def up_copy(step):
        slot = kv.at[level, head_of(step)]
        return remote(slot, slot, 1, step, in_sem.at[level, step], to_y)

    def own_half(which):
        hop, at = STEPS[1]
        slot = kv.at[level, 2 * x + at, which]
        return remote(slot, slot, 0, 1 - which, half_sem.at[which], (p, along(-hop)))

    def up_half(which):
        slot = kv.at[level, head_of(1), which]
        return remote(slot, slot, 1, 1 + which, in_sem.at[level, 1], to_y)

    def arrive_halves():
        for which in range(2):
            wait_in(kv.at[level, head_of(1), which], half_sem.at[which])
            up_half(which).start()
        up_copy(7).start()
        pl.when(even)(lambda: to_sibling(0, 1).start())

    def down_half(which):
        return remote(y_out.at[6, which], y_in.at[6, which], 9, 6 - 4 * which,
                      y_sem.at[6 - 4 * which], to_y)

    def x_half(which):
        return remote(x_out.at[6, which], x_in.at[6, which], 7, 6 - 6 * which, x_sem.at[6],
                      (p, along(STEPS[6][0])))

    def pass_x(step):
        hop, at = STEPS[step]
        slot = kv.at[up2, 2 * x + at]
        return remote(slot, slot, 2, step, in_sem.at[up2, step], (p, along(-hop)))

    def to_sibling(a, step):
        lev = up2 if a else level
        slot = kv.at[lev, head_of(step)]
        return remote(slot, slot, 3 + a, step, in_sem.at[lev, step], to_sib)

    def part_copy(n, step):
        return remote(sib_out.at[step, n], sib_in.at[step, n], 5 + n, step,
                      sib_sem.at[step, n], to_sib)

    def x_copy(step):
        return remote(x_out.at[step], x_in.at[step], 7, step, x_sem.at[step],
                      (p, along(hop_of(step))))

    def x_up_copy(step):
        hop, at = STEPS[step]
        return remote(x_out_up.at[at], x_in_up.at[at], 8, step, x_up_sem.at[at], (p, along(hop)))

    def down_copy(step):
        return remote(y_out.at[step], y_in.at[step], 9, step, y_sem.at[step], to_y)

    def wait_in(dst, sem):
        pltpu.make_async_remote_copy(
            src_ref=dst, dst_ref=dst, send_sem=out_sem.at[0, 0], recv_sem=sem,
            device_id=to_sib, device_id_type=MESH).wait_recv()

    def wait_kv(lev, step):
        wait_in(kv.at[lev, head_of(step)], in_sem.at[lev, step])

    def from_sibling(step):
        pl.when(level >= 1)(lambda: wait_kv(jnp.maximum(level - 1, 0), step))
        pl.when(level == 3)(lambda: wait_kv(jnp.int32(0), step))

    barrier = pltpu.get_barrier_semaphore()
    friends = [to_sib, to_y] + [(p, along(hop)) for hop in (1, 2, 3)]
    for device in friends:
        pl.semaphore_signal(barrier, inc=1, device_id=device, device_id_type=MESH)

    for which, ref in ((0, k_rows), (1, v_rows)):
        loads[which].wait()
        pair[...] = ref[...].astype(jnp.float32)
        for at in range(2):
            kv[level, 2 * x + at, which] = pair[pl.ds(at, TOK, stride=2), :].astype(jnp.bfloat16)
    pl.semaphore_wait(barrier, len(friends))

    def first_lower():
        up_copy(0).start()
        own_half(0).start()
        own_half(1).start()

    def first_even():
        to_sibling(0, 0).start()
        to_sibling(0, 7).start()

    pl.when(even)(first_even)
    pl.when(lower)(first_lower)
    pl.when(upper)(lambda: own_x(1).start())
    for step in (3, 2, 4):
        own_x(step).start()

    def blank():
        kv[3] = jnp.zeros((KVH, 2, TOK, HD), jnp.bfloat16)
    pl.when(level == 0)(blank)

    for at, (src, wide, dst) in enumerate(((q_rows, wide_o, qh), (g_rows, wide_q, gh))):
        loads[2 + at].wait()
        wide[...] = src[...].astype(jnp.float32)
        for head in range(KVH):
            for r in range(2):
                dst[head, r * TOK:(r + 1) * TOK, :] = (
                    wide[pl.ds(2 * head + r, TOK, stride=16), :].astype(jnp.bfloat16))

    loads[4].wait()
    lengths = []
    for k in range(LEVELS):
        real = lens[jnp.maximum(p - k, 0)]
        lengths.append(jnp.where(level >= k, real, 0))

    def compute(step, blocks):
        head = head_of(step)
        q = qh[head]
        g = gh[head]
        levs = [lax.rem(level - k + LEVELS, LEVELS) for k in range(blocks)]
        key_row = lax.broadcasted_iota(jnp.int32, (TOK, TOK), 0)
        query_tok = lax.broadcasted_iota(jnp.int32, (TOK, TOK), 1)
        floor = jnp.finfo(jnp.float32).min
        keys = jnp.concatenate([kv[lev, head, 0] for lev in levs], axis=0)
        vals = jnp.concatenate([kv[lev, head, 1] for lev in levs], axis=0)
        half_q = [q[r * TOK:(r + 1) * TOK] for r in range(2)]
        half_g = [g[r * TOK:(r + 1) * TOK] for r in range(2)]

        def block(got, k):
            return got[k * TOK:(k + 1) * TOK]

        def softmax(r, scores):
            tops, sums = [], []
            for k in range(blocks):
                seen = key_row < lengths[k]
                if k == 0:
                    seen = seen & (key_row <= query_tok)
                one = jnp.where(seen, block(scores, k) * SCORE_SCALE, -jnp.inf)
                high = jnp.maximum(jnp.max(one, axis=0, keepdims=True), floor)
                expo = jnp.exp2(one - high)
                score[r, k] = expo
                tops.append(high)
                sums.append(jnp.sum(expo, axis=0, keepdims=True))
            top = functools.reduce(jnp.maximum, tops)
            fades = [jnp.exp2(high - top) for high in tops]
            share = 1.0 / sum(one * fade for one, fade in zip(sums, fades))
            factors = [fade * share for fade in fades]
            for k in range(blocks):
                low[r, k] = (score[r, k] * factors[k]).astype(jnp.bfloat16)
            return factors

        def attend(r):
            weights = low[r, 0:blocks].reshape(blocks * TOK, TOK)
            return tn(vals, weights), nn(weights, half_g[r])

        def score_grads(r, out, dw, factors):
            turned = jnp.transpose(half_g[r].astype(jnp.float32))
            row_dot = jnp.sum(out * turned, axis=0, keepdims=True)
            for k in range(blocks):
                slope = (block(dw, k) - row_dot) * factors[k]
                ds[r, k] = (score[r, k] * slope).astype(jnp.bfloat16)

        def back(r):
            slopes = ds[r, 0:blocks].reshape(blocks * TOK, TOK)
            return tn(keys, slopes), nn(slopes, half_q[r])

        def give(r, out, dq):
            wide_o[pl.ds(2 * head + r, TOK, stride=16), :] = jnp.transpose(out)
            wide_q[pl.ds(2 * head + r, TOK, stride=16), :] = jnp.transpose(dq) * SCALE

        factors0 = softmax(0, nt(keys, half_q[0]))
        scores1 = nt(keys, half_q[1])
        out0, dv0 = attend(0)
        factors1 = softmax(1, scores1)
        dw0 = nt(vals, half_g[0])
        out1, dv1 = attend(1)
        score_grads(0, out0, dw0, factors0)
        dw1 = nt(vals, half_g[1])
        dq0, dk0 = back(0)
        score_grads(1, out1, dw1, factors1)
        dq1, dk1 = back(1)
        give(0, out0, dq0)
        give(1, out1, dq1)
        for k in range(blocks):
            for which, got in ((1, block(dv0, k) + block(dv1, k)),
                               (0, (block(dk0, k) + block(dk1, k)) * SCALE)):
                if k % 2 == 0:
                    part[step, k // 2, which] = got
                else:
                    sib_out[step, k // 2, which] = got.astype(jnp.bfloat16)

    def add_sibling(step):
        def add(a, n):
            wait_in(sib_in.at[step, n], sib_sem.at[step, n])
            part[step, a] = part[step, a] + sib_in[step, n].astype(jnp.float32)
        pl.when(even)(lambda: add(0, 0))
        pl.when(level == 3)(lambda: add(1, 0))
        pl.when(level == 2)(lambda: add(1, 1))

    def send_x(step):
        x_out[step] = part[step, 0].astype(jnp.bfloat16)
        x_copy(step).start()

    def finish_upper(step):
        add_sibling(step)
        direct = (step > 0) & (step < 6)
        for via in VIA_X:
            def along_x(via=via):
                x_out_up[STEPS[via][1]] = part[via, 1].astype(jnp.bfloat16)
                x_up_copy(via).start()
            pl.when(step == via)(along_x)
            direct = direct & (step != via)
        pl.when(direct)(lambda: send_down(step))

        def halves():
            for which in range(2):
                y_out[6, which] = part[6, 1, which].astype(jnp.bfloat16)
                down_half(which).start()
        pl.when(step == 6)(halves)
        pl.when((step > 0) & (step < 7))(lambda: send_x(step))

    def send_down(step):
        y_out[step] = part[step, 1].astype(jnp.bfloat16)
        down_copy(step).start()

    def pass_down(at):
        wait_in(x_in_up.at[at], x_up_sem.at[at])
        part[7 * at, 1] = part[7 * at, 1] + x_in_up[at].astype(jnp.float32)
        send_down(7 * at)

    def add_down(step):
        wait_in(y_in.at[step], y_sem.at[step])
        part[step, 0] = part[step, 0] + y_in[step].astype(jnp.float32)

    def take_down(step):
        direct = step > 0
        for via in VIA_X:
            direct = direct & (step != via)
        pl.when(direct)(lambda: add_down(step))
        send_x(step)

    def arrive_same(step):
        def body():
            wait_kv(level, step)
            pl.when(even)(lambda: to_sibling(0, step).start())
        pl.when((step > 0) & (step < 7))(body)

    def arrive_upper(step):
        def below():
            wait_kv(up2, step)
            to_sibling(1, step).start()

        def last_early():
            wait_kv(up2, 7)
            pass_x(VIA_X[1]).start()
            to_sibling(1, 7).start()

        pl.when(step < 7)(below)
        pl.when(step == 0)(lambda: pass_x(VIA_X[0]).start())
        pl.when(step == 1)(last_early)
        arrive_same(step)

    def step_upper(step):
        pl.when(step < 2)(lambda: own_x(step + 5).start())
        pl.when(step == 0)(lambda: arrive_upper(step))
        pl.when(step == 2)(lambda: arrive_upper(step))
        pl.when((step > 1) & (step < 6))(lambda: arrive_upper(step + 1))
        pl.when(step > 0)(lambda: finish_upper(step - 1))
        pl.when(step == 5)(lambda: pass_down(0))
        from_sibling(step)
        pl.when(level == 3)(lambda: compute(step, 4))
        pl.when(level == 2)(lambda: compute(step, 3))
        part_copy(0, step).start()
        pl.when(level == 3)(lambda: part_copy(1, step).start())
        pl.when(step == 0)(lambda: arrive_upper(step + 1))

    def step_lower(step):
        pl.when(step < 2)(lambda: own_x(step + 5).start())
        pl.when(step == 0)(arrive_halves)
        pl.when(step > 1)(lambda: arrive_same(step))
        pl.when((step > 1) & (step < 7) & (step != VIA_X[0]) & (step != VIA_X[1]))(
            lambda: up_copy(step).start())
        pl.when((step > 0) & even)(lambda: add_sibling(step - 1))
        from_sibling(step)
        compute(step, 2)
        pl.when(level == 1)(lambda: part_copy(0, step).start())

    def step_body(step, carry):
        pl.when(upper)(lambda: step_upper(step))
        pl.when(lower)(lambda: step_lower(step))
        return carry

    lax.fori_loop(0, 8, step_body, 0)

    def last_upper():
        finish_upper(jnp.int32(7))
        pass_down(1)

    def last_lower():
        pl.when(even)(lambda: add_sibling(jnp.int32(7)))

        def down_body(step, carry):
            take_down(step)
            return carry
        lax.fori_loop(1, 6, down_body, 0)
        for which in range(2):
            wait_in(y_in.at[6, which], y_sem.at[6 - 4 * which])
            x_out[6, which] = (
                part[6, 0, which] + y_in[6, which].astype(jnp.float32)).astype(jnp.bfloat16)
            x_half(which).start()

    pl.when(upper)(last_upper)
    q_rows[...] = wide_o[...].astype(jnp.bfloat16)
    g_rows[...] = wide_q[...].astype(jnp.bfloat16)
    stores = [
        pltpu.make_async_copy(src, dst, store_sem.at[at])
        for at, (src, dst) in enumerate((
            (q_rows, o_hbm), (g_rows, dq_hbm), (k_rows, dk_hbm), (v_rows, dv_hbm)))
    ]
    stores[0].start()
    stores[1].start()
    pl.when(lower)(last_lower)

    for at in range(2):
        mine = 7 * at
        for step in range(1, 7):
            if STEPS[step][1] == at:
                wait_in(x_in.at[step], x_sem.at[step])
                part[mine, 0] = part[mine, 0] + x_in[step].astype(jnp.float32)
        pl.when(lower)(functools.partial(add_down, mine))
    for which, ref in ((0, k_rows), (1, v_rows)):
        for at in range(2):
            pair[pl.ds(at, TOK, stride=2), :] = part[7 * at, 0, which]
        ref[...] = pair[...].astype(jnp.bfloat16)
        stores[2 + which].start()

    def sent_upper():
        for step in range(1, 7):
            own_x(step).wait_send()
            x_copy(step).wait_send()
        for step in range(8):
            to_sibling(1, step).wait_send()
            part_copy(0, step).wait_send()
        for step in (0, 1, 3, 5, 7):
            down_copy(step).wait_send()
        for which in range(2):
            down_half(which).wait_send()
        for step in VIA_X:
            pass_x(step).wait_send()
            x_up_copy(step).wait_send()

    def sent_lower():
        for step in range(2, 7):
            own_x(step).wait_send()
        for step in range(1, 6):
            x_copy(step).wait_send()
        for which in range(2):
            own_half(which).wait_send()
            up_half(which).wait_send()
            x_half(which).wait_send()
        for step in (0, 3, 5, 6, 7):
            up_copy(step).wait_send()

    pl.when(upper)(sent_upper)
    pl.when(lower)(sent_lower)
    for step in range(8):
        pl.when(even)(lambda step=step: to_sibling(0, step).wait_send())
        pl.when(level == 1)(lambda step=step: part_copy(0, step).wait_send())
        pl.when(level == 3)(lambda step=step: part_copy(1, step).wait_send())
    for store in stores:
        store.wait()


def unload(*refs):
    held, load_sem, store_sem = refs[8:12], refs[12], refs[13]
    moves = []
    for at in range(4):
        rows = refs[at].shape[0] // UNLOADS
        for piece in range(UNLOADS):
            cut = pl.ds(piece * rows, rows)
            moves.append((
                pltpu.make_async_copy(refs[at].at[cut], held[at].at[cut], load_sem.at[at, piece]),
                pltpu.make_async_copy(held[at].at[cut], refs[4 + at].at[cut], store_sem.at[at, piece])))
    for load, _ in moves:
        load.start()
    for load, store in moves:
        load.wait()
        store.start()
    for _, store in moves:
        store.wait()


def shards(queries, keys, values, grad_out, parents, node_lengths):
    del parents
    tokens = queries.shape[0]
    wide_rows = tokens * KVH * 2
    hbm = pl.BlockSpec(memory_space=pltpu.HBM)
    out = pl.pallas_call(
        kernel,
        out_shape=(
            jax.ShapeDtypeStruct((wide_rows, HD), jnp.bfloat16),
            jax.ShapeDtypeStruct((wide_rows, HD), jnp.bfloat16),
            jax.ShapeDtypeStruct((2 * tokens, HD), jnp.bfloat16),
            jax.ShapeDtypeStruct((2 * tokens, HD), jnp.bfloat16),
        ),
        in_specs=[hbm] * 5,
        out_specs=(hbm,) * 4,
        scratch_shapes=[
            pltpu.VMEM((wide_rows, HD), jnp.bfloat16),
            pltpu.VMEM((wide_rows, HD), jnp.bfloat16),
            pltpu.VMEM((2 * tokens, HD), jnp.bfloat16),
            pltpu.VMEM((2 * tokens, HD), jnp.bfloat16),
            pltpu.SMEM(node_lengths.shape, jnp.int32),
            pltpu.VMEM((LEVELS, KVH, 2, TOK, HD), jnp.bfloat16),
            pltpu.VMEM((KVH, ROWS, HD), jnp.bfloat16),
            pltpu.VMEM((KVH, ROWS, HD), jnp.bfloat16),
            pltpu.VMEM((wide_rows, HD), jnp.float32),
            pltpu.VMEM((wide_rows, HD), jnp.float32),
            pltpu.VMEM((2 * tokens, HD), jnp.float32),
            pltpu.VMEM((2, LEVELS, TOK, TOK), jnp.float32),
            pltpu.VMEM((2, LEVELS, TOK, TOK), jnp.bfloat16),
            pltpu.VMEM((2, LEVELS, TOK, TOK), jnp.bfloat16),
            pltpu.VMEM((8, 2, 2, TOK, HD), jnp.float32),
            pltpu.VMEM((8, 2, 2, TOK, HD), jnp.bfloat16),
            pltpu.VMEM((8, 2, 2, TOK, HD), jnp.bfloat16),
            pltpu.VMEM((8, 2, TOK, HD), jnp.bfloat16),
            pltpu.VMEM((8, 2, TOK, HD), jnp.bfloat16),
            pltpu.VMEM((8, 2, TOK, HD), jnp.bfloat16),
            pltpu.VMEM((8, 2, TOK, HD), jnp.bfloat16),
            pltpu.VMEM((2, 2, TOK, HD), jnp.bfloat16),
            pltpu.VMEM((2, 2, TOK, HD), jnp.bfloat16),
            pltpu.SemaphoreType.DMA((5,)),
            pltpu.SemaphoreType.DMA((4,)),
            pltpu.SemaphoreType.DMA((2,)),
            pltpu.SemaphoreType.DMA((LEVELS, 8)),
            pltpu.SemaphoreType.DMA((10, 8)),
            pltpu.SemaphoreType.DMA((8, 2)),
            pltpu.SemaphoreType.DMA((8,)),
            pltpu.SemaphoreType.DMA((2,)),
            pltpu.SemaphoreType.DMA((8,)),
        ],
        compiler_params=pltpu.CompilerParams(
            collective_id=0, has_side_effects=True, vmem_limit_bytes=VMEM_BYTES),
        cost_estimate=pl.CostEstimate(
            flops=12 * 16 * TOK * 4 * TOK * HD, bytes_accessed=5 * 1024 * 1024,
            transcendentals=16 * TOK * 4 * TOK),
    )(
        queries.reshape(wide_rows, HD),
        grad_out.reshape(wide_rows, HD),
        keys.reshape(2 * tokens, HD),
        values.reshape(2 * tokens, HD),
        node_lengths,
    )
    out = pl.pallas_call(
        unload,
        out_shape=tuple(jax.ShapeDtypeStruct(one.shape, one.dtype) for one in out),
        in_specs=[hbm] * 4,
        out_specs=(hbm,) * 4,
        scratch_shapes=[pltpu.VMEM(one.shape, one.dtype) for one in out]
        + [pltpu.SemaphoreType.DMA((4, UNLOADS))] * 2,
        compiler_params=pltpu.CompilerParams(vmem_limit_bytes=VMEM_BYTES),
    )(*out)
    return (
        out[0].reshape(queries.shape),
        out[1].reshape(queries.shape),
        out[2].reshape(keys.shape),
        out[3].reshape(values.shape),
    )


def solution(mesh):
    in_specs = (
        P("node", None, "head", None),
        P("node", "head", None),
        P("node", "head", None),
        P("node", None, "head", None),
        P(),
        P(),
    )
    out_specs = (
        P("node", None, "head", None),
        P("node", None, "head", None),
        P("node", "head", None),
        P("node", "head", None),
    )
    return jax.shard_map(shards, mesh=mesh, in_specs=in_specs, out_specs=out_specs, check_vma=False)
```

```python
import functools
import math

import jax
import jax.numpy as jnp
from jax import lax
from jax.experimental import pallas as pl
from jax.experimental.pallas import tpu as pltpu
from jax.sharding import PartitionSpec as P

MESH = pl.DeviceIdType.MESH
VMEM_BYTES = 63 * 1024 * 1024
UNLOADS = 2
TOK = 256
LEVELS = 4
KVH = 8
HD = 128
ROWS = 512
SCALE = HD ** -0.5
SCORE_SCALE = SCALE * math.log2(math.e)

STEPS = ((0, 0), (1, 0), (3, 0), (2, 1), (1, 1), (2, 0), (3, 1), (0, 1))
VIA_X = (2, 4)
SEND_UPPER = ((2,), (4, 3), (6, 5))
SEND_LOWER = ((2, 4), (3, 6), (5,))


def nt(a, b):
    return lax.dot_general(a, b, (((1,), (1,)), ((), ())), preferred_element_type=jnp.float32)


def tn(a, b):
    return lax.dot_general(a, b, (((0,), (0,)), ((), ())), preferred_element_type=jnp.float32)


def nn(a, b):
    return lax.dot_general(a, b, (((1,), (0,)), ((), ())), preferred_element_type=jnp.float32)


def table(step, values):
    picked = jnp.int32(values[0])
    for at in range(1, len(values)):
        picked = jnp.where(step == at, jnp.int32(values[at]), picked)
    return picked


def kernel(
    q_hbm, g_hbm, k_hbm, v_hbm, len_hbm,
    o_hbm, dq_hbm, dk_hbm, dv_hbm,
    q_rows, g_rows, k_rows, v_rows, lens,
    kv, qh, gh, wide_o, wide_q, pair, score, low, ds, part,
    sib_out, sib_in, x_out, x_in, y_out, y_in, x_out_up, x_in_up,
    load_sem, store_sem, half_sem, in_sem, out_sem, sib_sem, x_sem, x_up_sem, y_sem,
):
    loads = [
        pltpu.make_async_copy(src, dst, load_sem.at[at])
        for at, (src, dst) in enumerate((
            (k_hbm, k_rows), (v_hbm, v_rows), (q_hbm, q_rows), (g_hbm, g_rows), (len_hbm, lens)))
    ]
    for load in loads:
        load.start()
    p = lax.axis_index("node")
    x = lax.axis_index("head")
    level = lax.rem(p, LEVELS)
    odd = lax.rem(p, 2)
    upper = level >= 2
    lower = level < 2
    even = odd == 0
    up2 = jnp.maximum(level - 2, 0)
    y_node = p + 2 - 4 * (level // 2)
    to_sib = (p + 1 - 2 * odd, x)
    to_y = (y_node, x)

    def along(distance):
        return lax.rem(x + distance + 4, 4)

    def hop_of(step):
        return table(step, [hop for hop, _ in STEPS])

    def head_of(step):
        return 2 * along(hop_of(step)) + table(step, [at for _, at in STEPS])

    def remote(src, dst, kind, step, sem, device):
        return pltpu.make_async_remote_copy(
            src_ref=src, dst_ref=dst, send_sem=out_sem.at[kind, step], recv_sem=sem,
            device_id=device, device_id_type=MESH)

    def own_x(step):
        slot = kv.at[level, 2 * x + table(step, [at for _, at in STEPS])]
        return remote(slot, slot, 0, step, in_sem.at[level, step], (p, along(-hop_of(step))))

    def up_copy(step):
        slot = kv.at[level, head_of(step)]
        return remote(slot, slot, 1, step, in_sem.at[level, step], to_y)

    def own_half(which):
        hop, at = STEPS[1]
        slot = kv.at[level, 2 * x + at, which]
        return remote(slot, slot, 0, 1 - which, half_sem.at[which], (p, along(-hop)))

    def up_half(which):
        slot = kv.at[level, head_of(1), which]
        return remote(slot, slot, 1, 1 + which, in_sem.at[level, 1], to_y)

    def arrive_halves():
        for which in range(2):
            wait_in(kv.at[level, head_of(1), which], half_sem.at[which])
            up_half(which).start()
        up_copy(7).start()
        pl.when(even)(lambda: to_sibling(0, 1).start())

    def down_half(which):
        return remote(y_out.at[6, which], y_in.at[6, which], 9, 6 - 4 * which,
                      y_sem.at[6 - 4 * which], to_y)

    def x_half(which):
        return remote(x_out.at[6, which], x_in.at[6, which], 7, 6 - 6 * which, x_sem.at[6],
                      (p, along(STEPS[6][0])))

    def pass_x(step):
        hop, at = STEPS[step]
        slot = kv.at[up2, 2 * x + at]
        return remote(slot, slot, 2, step, in_sem.at[up2, step], (p, along(-hop)))

    def to_sibling(a, step):
        lev = up2 if a else level
        slot = kv.at[lev, head_of(step)]
        return remote(slot, slot, 3 + a, step, in_sem.at[lev, step], to_sib)

    def part_copy(n, step):
        return remote(sib_out.at[step, n], sib_in.at[step, n], 5 + n, step,
                      sib_sem.at[step, n], to_sib)

    def x_copy(step):
        return remote(x_out.at[step], x_in.at[step], 7, step, x_sem.at[step],
                      (p, along(hop_of(step))))

    def x_up_copy(step):
        hop, at = STEPS[step]
        return remote(x_out_up.at[at], x_in_up.at[at], 8, step, x_up_sem.at[at], (p, along(hop)))

    def down_copy(step):
        return remote(y_out.at[step], y_in.at[step], 9, step, y_sem.at[step], to_y)

    def wait_in(dst, sem):
        pltpu.make_async_remote_copy(
            src_ref=dst, dst_ref=dst, send_sem=out_sem.at[0, 0], recv_sem=sem,
            device_id=to_sib, device_id_type=MESH).wait_recv()

    def wait_kv(lev, step):
        wait_in(kv.at[lev, head_of(step)], in_sem.at[lev, step])

    def from_sibling(step):
        pl.when(level >= 1)(lambda: wait_kv(jnp.maximum(level - 1, 0), step))
        pl.when(level == 3)(lambda: wait_kv(jnp.int32(0), step))

    barrier = pltpu.get_barrier_semaphore()
    friends = [to_sib, to_y] + [(p, along(hop)) for hop in (1, 2, 3)]
    for device in friends:
        pl.semaphore_signal(barrier, inc=1, device_id=device, device_id_type=MESH)

    for which, ref in ((0, k_rows), (1, v_rows)):
        loads[which].wait()
        pair[...] = ref[...].astype(jnp.float32)
        for at in range(2):
            kv[level, 2 * x + at, which] = pair[pl.ds(at, TOK, stride=2), :].astype(jnp.bfloat16)
    pl.semaphore_wait(barrier, len(friends))

    def first_lower():
        up_copy(0).start()
        own_half(0).start()
        own_half(1).start()

    def first_even():
        to_sibling(0, 0).start()
        to_sibling(0, 7).start()

    pl.when(even)(first_even)
    pl.when(lower)(first_lower)
    pl.when(upper)(lambda: own_x(1).start())
    for cond, plan in ((upper, SEND_UPPER), (lower, SEND_LOWER)):
        def send_first(plan=plan):
            for step in plan[0]:
                own_x(step).start()
        pl.when(cond)(send_first)

    def blank():
        kv[3] = jnp.zeros((KVH, 2, TOK, HD), jnp.bfloat16)
    pl.when(level == 0)(blank)

    for at, (src, wide, dst) in enumerate(((q_rows, wide_o, qh), (g_rows, wide_q, gh))):
        loads[2 + at].wait()
        wide[...] = src[...].astype(jnp.float32)
        for head in range(KVH):
            for r in range(2):
                dst[head, r * TOK:(r + 1) * TOK, :] = (
                    wide[pl.ds(2 * head + r, TOK, stride=16), :].astype(jnp.bfloat16))

    loads[4].wait()
    lengths = []
    for k in range(LEVELS):
        real = lens[jnp.maximum(p - k, 0)]
        lengths.append(jnp.where(level >= k, real, 0))

    def compute(step, blocks):
        head = head_of(step)
        q = qh[head]
        g = gh[head]
        levs = [lax.rem(level - k + LEVELS, LEVELS) for k in range(blocks)]
        key_row = lax.broadcasted_iota(jnp.int32, (TOK, TOK), 0)
        query_tok = lax.broadcasted_iota(jnp.int32, (TOK, TOK), 1)
        floor = jnp.finfo(jnp.float32).min
        keys = jnp.concatenate([kv[lev, head, 0] for lev in levs], axis=0)
        vals = jnp.concatenate([kv[lev, head, 1] for lev in levs], axis=0)
        half_q = [q[r * TOK:(r + 1) * TOK] for r in range(2)]
        half_g = [g[r * TOK:(r + 1) * TOK] for r in range(2)]

        def block(got, k):
            return got[k * TOK:(k + 1) * TOK]

        def softmax(r, scores):
            tops, sums = [], []
            for k in range(blocks):
                seen = key_row < lengths[k]
                if k == 0:
                    seen = seen & (key_row <= query_tok)
                one = jnp.where(seen, block(scores, k) * SCORE_SCALE, -jnp.inf)
                high = jnp.maximum(jnp.max(one, axis=0, keepdims=True), floor)
                expo = jnp.exp2(one - high)
                score[r, k] = expo
                tops.append(high)
                sums.append(jnp.sum(expo, axis=0, keepdims=True))
            top = functools.reduce(jnp.maximum, tops)
            fades = [jnp.exp2(high - top) for high in tops]
            share = 1.0 / sum(one * fade for one, fade in zip(sums, fades))
            factors = [fade * share for fade in fades]
            for k in range(blocks):
                low[r, k] = (score[r, k] * factors[k]).astype(jnp.bfloat16)
            return factors

        def attend(r):
            weights = low[r, 0:blocks].reshape(blocks * TOK, TOK)
            return tn(vals, weights), nn(weights, half_g[r])

        def score_grads(r, out, dw, factors):
            turned = jnp.transpose(half_g[r].astype(jnp.float32))
            row_dot = jnp.sum(out * turned, axis=0, keepdims=True)
            for k in range(blocks):
                slope = (block(dw, k) - row_dot) * factors[k]
                ds[r, k] = (score[r, k] * slope).astype(jnp.bfloat16)

        def back(r):
            slopes = ds[r, 0:blocks].reshape(blocks * TOK, TOK)
            return tn(keys, slopes), nn(slopes, half_q[r])

        def give(r, out, dq):
            wide_o[pl.ds(2 * head + r, TOK, stride=16), :] = jnp.transpose(out)
            wide_q[pl.ds(2 * head + r, TOK, stride=16), :] = jnp.transpose(dq) * SCALE

        factors0 = softmax(0, nt(keys, half_q[0]))
        scores1 = nt(keys, half_q[1])
        out0, dv0 = attend(0)
        factors1 = softmax(1, scores1)
        dw0 = nt(vals, half_g[0])
        out1, dv1 = attend(1)
        score_grads(0, out0, dw0, factors0)
        dw1 = nt(vals, half_g[1])
        dq0, dk0 = back(0)
        score_grads(1, out1, dw1, factors1)
        dq1, dk1 = back(1)
        give(0, out0, dq0)
        give(1, out1, dq1)
        for k in range(blocks):
            for which, got in ((1, block(dv0, k) + block(dv1, k)),
                               (0, (block(dk0, k) + block(dk1, k)) * SCALE)):
                if k % 2 == 0:
                    part[step, k // 2, which] = got
                else:
                    sib_out[step, k // 2, which] = got.astype(jnp.bfloat16)

    def add_sibling(step):
        def add(a, n):
            wait_in(sib_in.at[step, n], sib_sem.at[step, n])
            part[step, a] = part[step, a] + sib_in[step, n].astype(jnp.float32)
        pl.when(even)(lambda: add(0, 0))
        pl.when(level == 3)(lambda: add(1, 0))
        pl.when(level == 2)(lambda: add(1, 1))

    def send_x(step):
        x_out[step] = part[step, 0].astype(jnp.bfloat16)
        x_copy(step).start()

    def finish_upper(step):
        add_sibling(step)
        direct = (step > 0) & (step < 6)
        for via in VIA_X:
            def along_x(via=via):
                x_out_up[STEPS[via][1]] = part[via, 1].astype(jnp.bfloat16)
                x_up_copy(via).start()
            pl.when(step == via)(along_x)
            direct = direct & (step != via)
        pl.when(direct)(lambda: send_down(step))

        def halves():
            for which in range(2):
                y_out[6, which] = part[6, 1, which].astype(jnp.bfloat16)
                down_half(which).start()
        pl.when(step == 6)(halves)
        pl.when((step > 0) & (step < 7))(lambda: send_x(step))

    def send_down(step):
        y_out[step] = part[step, 1].astype(jnp.bfloat16)
        down_copy(step).start()

    def pass_down(at):
        wait_in(x_in_up.at[at], x_up_sem.at[at])
        part[7 * at, 1] = part[7 * at, 1] + x_in_up[at].astype(jnp.float32)
        send_down(7 * at)

    def add_down(step):
        wait_in(y_in.at[step], y_sem.at[step])
        part[step, 0] = part[step, 0] + y_in[step].astype(jnp.float32)

    def take_down(step):
        direct = step > 0
        for via in VIA_X:
            direct = direct & (step != via)
        pl.when(direct)(lambda: add_down(step))
        send_x(step)

    def arrive_same(step):
        def body():
            wait_kv(level, step)
            pl.when(even)(lambda: to_sibling(0, step).start())
        pl.when((step > 0) & (step < 7))(body)

    def arrive_upper(step):
        def below():
            wait_kv(up2, step)
            to_sibling(1, step).start()

        def last_early():
            wait_kv(up2, 7)
            pass_x(VIA_X[1]).start()
            to_sibling(1, 7).start()

        pl.when(step < 7)(below)
        pl.when(step == 0)(lambda: pass_x(VIA_X[0]).start())
        pl.when(step == 1)(last_early)
        arrive_same(step)

    def send_own(step, plan):
        for at, sent in enumerate(plan[1:]):
            def go(sent=sent):
                for one in sent:
                    own_x(one).start()
            pl.when(step == at)(go)

    def step_upper(step):
        send_own(step, SEND_UPPER)
        pl.when(step == 0)(lambda: arrive_upper(step))
        pl.when(step == 2)(lambda: arrive_upper(step))
        pl.when((step > 1) & (step < 6))(lambda: arrive_upper(step + 1))
        pl.when(step > 0)(lambda: finish_upper(step - 1))
        pl.when(step == 5)(lambda: pass_down(0))
        from_sibling(step)
        pl.when(level == 3)(lambda: compute(step, 4))
        pl.when(level == 2)(lambda: compute(step, 3))
        part_copy(0, step).start()
        pl.when(level == 3)(lambda: part_copy(1, step).start())
        pl.when(step == 0)(lambda: arrive_upper(step + 1))

    def step_lower(step):
        send_own(step, SEND_LOWER)
        pl.when(step == 0)(arrive_halves)
        pl.when(step > 1)(lambda: arrive_same(step))
        pl.when((step > 1) & (step < 7) & (step != VIA_X[0]) & (step != VIA_X[1]))(
            lambda: up_copy(step).start())
        pl.when((step > 0) & even)(lambda: add_sibling(step - 1))
        from_sibling(step)
        compute(step, 2)
        pl.when(level == 1)(lambda: part_copy(0, step).start())

    def step_body(step, carry):
        pl.when(upper)(lambda: step_upper(step))
        pl.when(lower)(lambda: step_lower(step))
        return carry

    lax.fori_loop(0, 8, step_body, 0)

    def last_upper():
        finish_upper(jnp.int32(7))
        pass_down(1)

    def last_lower():
        pl.when(even)(lambda: add_sibling(jnp.int32(7)))

        def down_body(step, carry):
            take_down(step)
            return carry
        lax.fori_loop(1, 6, down_body, 0)
        for which in range(2):
            wait_in(y_in.at[6, which], y_sem.at[6 - 4 * which])
            x_out[6, which] = (
                part[6, 0, which] + y_in[6, which].astype(jnp.float32)).astype(jnp.bfloat16)
            x_half(which).start()

    pl.when(upper)(last_upper)
    q_rows[...] = wide_o[...].astype(jnp.bfloat16)
    g_rows[...] = wide_q[...].astype(jnp.bfloat16)
    stores = [
        pltpu.make_async_copy(src, dst, store_sem.at[at])
        for at, (src, dst) in enumerate((
            (q_rows, o_hbm), (g_rows, dq_hbm), (k_rows, dk_hbm), (v_rows, dv_hbm)))
    ]
    stores[0].start()
    stores[1].start()
    pl.when(lower)(last_lower)

    for at in range(2):
        mine = 7 * at
        for step in range(1, 7):
            if STEPS[step][1] == at:
                wait_in(x_in.at[step], x_sem.at[step])
                part[mine, 0] = part[mine, 0] + x_in[step].astype(jnp.float32)
        pl.when(lower)(functools.partial(add_down, mine))
    for which, ref in ((0, k_rows), (1, v_rows)):
        for at in range(2):
            pair[pl.ds(at, TOK, stride=2), :] = part[7 * at, 0, which]
        ref[...] = pair[...].astype(jnp.bfloat16)
        stores[2 + which].start()

    def sent_upper():
        for step in range(1, 7):
            own_x(step).wait_send()
            x_copy(step).wait_send()
        for step in range(8):
            to_sibling(1, step).wait_send()
            part_copy(0, step).wait_send()
        for step in (0, 1, 3, 5, 7):
            down_copy(step).wait_send()
        for which in range(2):
            down_half(which).wait_send()
        for step in VIA_X:
            pass_x(step).wait_send()
            x_up_copy(step).wait_send()

    def sent_lower():
        for step in range(2, 7):
            own_x(step).wait_send()
        for step in range(1, 6):
            x_copy(step).wait_send()
        for which in range(2):
            own_half(which).wait_send()
            up_half(which).wait_send()
            x_half(which).wait_send()
        for step in (0, 3, 5, 6, 7):
            up_copy(step).wait_send()

    pl.when(upper)(sent_upper)
    pl.when(lower)(sent_lower)
    for step in range(8):
        pl.when(even)(lambda step=step: to_sibling(0, step).wait_send())
        pl.when(level == 1)(lambda step=step: part_copy(0, step).wait_send())
        pl.when(level == 3)(lambda step=step: part_copy(1, step).wait_send())
    for store in stores:
        store.wait()


def unload(*refs):
    held, load_sem, store_sem = refs[8:12], refs[12], refs[13]
    moves = []
    for at in range(4):
        rows = refs[at].shape[0] // UNLOADS
        for piece in range(UNLOADS):
            cut = pl.ds(piece * rows, rows)
            moves.append((
                pltpu.make_async_copy(refs[at].at[cut], held[at].at[cut], load_sem.at[at, piece]),
                pltpu.make_async_copy(held[at].at[cut], refs[4 + at].at[cut], store_sem.at[at, piece])))
    for load, _ in moves:
        load.start()
    for load, store in moves:
        load.wait()
        store.start()
    for _, store in moves:
        store.wait()


def shards(queries, keys, values, grad_out, parents, node_lengths):
    del parents
    tokens = queries.shape[0]
    wide_rows = tokens * KVH * 2
    hbm = pl.BlockSpec(memory_space=pltpu.HBM)
    out = pl.pallas_call(
        kernel,
        out_shape=(
            jax.ShapeDtypeStruct((wide_rows, HD), jnp.bfloat16),
            jax.ShapeDtypeStruct((wide_rows, HD), jnp.bfloat16),
            jax.ShapeDtypeStruct((2 * tokens, HD), jnp.bfloat16),
            jax.ShapeDtypeStruct((2 * tokens, HD), jnp.bfloat16),
        ),
        in_specs=[hbm] * 5,
        out_specs=(hbm,) * 4,
        scratch_shapes=[
            pltpu.VMEM((wide_rows, HD), jnp.bfloat16),
            pltpu.VMEM((wide_rows, HD), jnp.bfloat16),
            pltpu.VMEM((2 * tokens, HD), jnp.bfloat16),
            pltpu.VMEM((2 * tokens, HD), jnp.bfloat16),
            pltpu.SMEM(node_lengths.shape, jnp.int32),
            pltpu.VMEM((LEVELS, KVH, 2, TOK, HD), jnp.bfloat16),
            pltpu.VMEM((KVH, ROWS, HD), jnp.bfloat16),
            pltpu.VMEM((KVH, ROWS, HD), jnp.bfloat16),
            pltpu.VMEM((wide_rows, HD), jnp.float32),
            pltpu.VMEM((wide_rows, HD), jnp.float32),
            pltpu.VMEM((2 * tokens, HD), jnp.float32),
            pltpu.VMEM((2, LEVELS, TOK, TOK), jnp.float32),
            pltpu.VMEM((2, LEVELS, TOK, TOK), jnp.bfloat16),
            pltpu.VMEM((2, LEVELS, TOK, TOK), jnp.bfloat16),
            pltpu.VMEM((8, 2, 2, TOK, HD), jnp.float32),
            pltpu.VMEM((8, 2, 2, TOK, HD), jnp.bfloat16),
            pltpu.VMEM((8, 2, 2, TOK, HD), jnp.bfloat16),
            pltpu.VMEM((8, 2, TOK, HD), jnp.bfloat16),
            pltpu.VMEM((8, 2, TOK, HD), jnp.bfloat16),
            pltpu.VMEM((8, 2, TOK, HD), jnp.bfloat16),
            pltpu.VMEM((8, 2, TOK, HD), jnp.bfloat16),
            pltpu.VMEM((2, 2, TOK, HD), jnp.bfloat16),
            pltpu.VMEM((2, 2, TOK, HD), jnp.bfloat16),
            pltpu.SemaphoreType.DMA((5,)),
            pltpu.SemaphoreType.DMA((4,)),
            pltpu.SemaphoreType.DMA((2,)),
            pltpu.SemaphoreType.DMA((LEVELS, 8)),
            pltpu.SemaphoreType.DMA((10, 8)),
            pltpu.SemaphoreType.DMA((8, 2)),
            pltpu.SemaphoreType.DMA((8,)),
            pltpu.SemaphoreType.DMA((2,)),
            pltpu.SemaphoreType.DMA((8,)),
        ],
        compiler_params=pltpu.CompilerParams(
            collective_id=0, has_side_effects=True, vmem_limit_bytes=VMEM_BYTES),
        cost_estimate=pl.CostEstimate(
            flops=12 * 16 * TOK * 4 * TOK * HD, bytes_accessed=5 * 1024 * 1024,
            transcendentals=16 * TOK * 4 * TOK),
    )(
        queries.reshape(wide_rows, HD),
        grad_out.reshape(wide_rows, HD),
        keys.reshape(2 * tokens, HD),
        values.reshape(2 * tokens, HD),
        node_lengths,
    )
    out = pl.pallas_call(
        unload,
        out_shape=tuple(jax.ShapeDtypeStruct(one.shape, one.dtype) for one in out),
        in_specs=[hbm] * 4,
        out_specs=(hbm,) * 4,
        scratch_shapes=[pltpu.VMEM(one.shape, one.dtype) for one in out]
        + [pltpu.SemaphoreType.DMA((4, UNLOADS))] * 2,
        compiler_params=pltpu.CompilerParams(vmem_limit_bytes=VMEM_BYTES),
    )(*out)
    return (
        out[0].reshape(queries.shape),
        out[1].reshape(queries.shape),
        out[2].reshape(keys.shape),
        out[3].reshape(values.shape),
    )


def solution(mesh):
    in_specs = (
        P("node", None, "head", None),
        P("node", "head", None),
        P("node", "head", None),
        P("node", None, "head", None),
        P(),
        P(),
    )
    out_specs = (
        P("node", None, "head", None),
        P("node", None, "head", None),
        P("node", "head", None),
        P("node", "head", None),
    )
    return jax.shard_map(shards, mesh=mesh, in_specs=in_specs, out_specs=out_specs, check_vma=False)
```

```python
import functools
import math

import jax
import jax.numpy as jnp
from jax import lax
from jax.experimental import pallas as pl
from jax.experimental.pallas import tpu as pltpu
from jax.sharding import PartitionSpec as P

MESH = pl.DeviceIdType.MESH
VMEM_BYTES = 63 * 1024 * 1024
UNLOADS = 2
TOK = 256
LEVELS = 4
KVH = 8
HD = 128
ROWS = 512
SCALE = HD ** -0.5
SCORE_SCALE = SCALE * math.log2(math.e)

STEPS = ((0, 0), (1, 0), (3, 0), (2, 1), (1, 1), (2, 0), (3, 1), (0, 1))
VIA_X = (2, 4)
SEND_UPPER = ((2,), (4, 3), (6, 5))
SEND_LOWER = ((2,), (3, 6), (5, 4))


def nt(a, b):
    return lax.dot_general(a, b, (((1,), (1,)), ((), ())), preferred_element_type=jnp.float32)


def tn(a, b):
    return lax.dot_general(a, b, (((0,), (0,)), ((), ())), preferred_element_type=jnp.float32)


def nn(a, b):
    return lax.dot_general(a, b, (((1,), (0,)), ((), ())), preferred_element_type=jnp.float32)


def table(step, values):
    picked = jnp.int32(values[0])
    for at in range(1, len(values)):
        picked = jnp.where(step == at, jnp.int32(values[at]), picked)
    return picked


def kernel(
    q_hbm, g_hbm, k_hbm, v_hbm, len_hbm,
    o_hbm, dq_hbm, dk_hbm, dv_hbm,
    q_rows, g_rows, k_rows, v_rows, lens,
    kv, qh, gh, wide_o, wide_q, pair, score, low, ds, part,
    sib_out, sib_in, x_out, x_in, y_out, y_in, x_out_up, x_in_up,
    load_sem, store_sem, half_sem, in_sem, out_sem, sib_sem, x_sem, x_up_sem, y_sem,
):
    loads = [
        pltpu.make_async_copy(src, dst, load_sem.at[at])
        for at, (src, dst) in enumerate((
            (k_hbm, k_rows), (v_hbm, v_rows), (q_hbm, q_rows), (g_hbm, g_rows), (len_hbm, lens)))
    ]
    for load in loads:
        load.start()
    p = lax.axis_index("node")
    x = lax.axis_index("head")
    level = lax.rem(p, LEVELS)
    odd = lax.rem(p, 2)
    upper = level >= 2
    lower = level < 2
    even = odd == 0
    up2 = jnp.maximum(level - 2, 0)
    y_node = p + 2 - 4 * (level // 2)
    to_sib = (p + 1 - 2 * odd, x)
    to_y = (y_node, x)

    def along(distance):
        return lax.rem(x + distance + 4, 4)

    def hop_of(step):
        return table(step, [hop for hop, _ in STEPS])

    def head_of(step):
        return 2 * along(hop_of(step)) + table(step, [at for _, at in STEPS])

    def remote(src, dst, kind, step, sem, device):
        return pltpu.make_async_remote_copy(
            src_ref=src, dst_ref=dst, send_sem=out_sem.at[kind, step], recv_sem=sem,
            device_id=device, device_id_type=MESH)

    def own_x(step):
        slot = kv.at[level, 2 * x + table(step, [at for _, at in STEPS])]
        return remote(slot, slot, 0, step, in_sem.at[level, step], (p, along(-hop_of(step))))

    def up_copy(step):
        slot = kv.at[level, head_of(step)]
        return remote(slot, slot, 1, step, in_sem.at[level, step], to_y)

    def own_half(which):
        hop, at = STEPS[1]
        slot = kv.at[level, 2 * x + at, which]
        return remote(slot, slot, 0, 1 - which, half_sem.at[which], (p, along(-hop)))

    def up_half(which):
        slot = kv.at[level, head_of(1), which]
        return remote(slot, slot, 1, 1 + which, in_sem.at[level, 1], to_y)

    def arrive_halves():
        for which in range(2):
            wait_in(kv.at[level, head_of(1), which], half_sem.at[which])
            up_half(which).start()
        up_copy(7).start()
        pl.when(even)(lambda: to_sibling(0, 1).start())

    def down_half(which):
        return remote(y_out.at[6, which], y_in.at[6, which], 9, 6 - 4 * which,
                      y_sem.at[6 - 4 * which], to_y)

    def x_half(which):
        return remote(x_out.at[6, which], x_in.at[6, which], 7, 6 - 6 * which, x_sem.at[6],
                      (p, along(STEPS[6][0])))

    def pass_x(step):
        hop, at = STEPS[step]
        slot = kv.at[up2, 2 * x + at]
        return remote(slot, slot, 2, step, in_sem.at[up2, step], (p, along(-hop)))

    def to_sibling(a, step):
        lev = up2 if a else level
        slot = kv.at[lev, head_of(step)]
        return remote(slot, slot, 3 + a, step, in_sem.at[lev, step], to_sib)

    def part_copy(n, step):
        return remote(sib_out.at[step, n], sib_in.at[step, n], 5 + n, step,
                      sib_sem.at[step, n], to_sib)

    def x_copy(step):
        return remote(x_out.at[step], x_in.at[step], 7, step, x_sem.at[step],
                      (p, along(hop_of(step))))

    def x_up_copy(step):
        hop, at = STEPS[step]
        return remote(x_out_up.at[at], x_in_up.at[at], 8, step, x_up_sem.at[at], (p, along(hop)))

    def down_copy(step):
        return remote(y_out.at[step], y_in.at[step], 9, step, y_sem.at[step], to_y)

    def wait_in(dst, sem):
        pltpu.make_async_remote_copy(
            src_ref=dst, dst_ref=dst, send_sem=out_sem.at[0, 0], recv_sem=sem,
            device_id=to_sib, device_id_type=MESH).wait_recv()

    def wait_kv(lev, step):
        wait_in(kv.at[lev, head_of(step)], in_sem.at[lev, step])

    def from_sibling(step):
        pl.when(level >= 1)(lambda: wait_kv(jnp.maximum(level - 1, 0), step))
        pl.when(level == 3)(lambda: wait_kv(jnp.int32(0), step))

    barrier = pltpu.get_barrier_semaphore()
    friends = [to_sib, to_y] + [(p, along(hop)) for hop in (1, 2, 3)]
    for device in friends:
        pl.semaphore_signal(barrier, inc=1, device_id=device, device_id_type=MESH)

    for which, ref in ((0, k_rows), (1, v_rows)):
        loads[which].wait()
        pair[...] = ref[...].astype(jnp.float32)
        for at in range(2):
            kv[level, 2 * x + at, which] = pair[pl.ds(at, TOK, stride=2), :].astype(jnp.bfloat16)
    pl.semaphore_wait(barrier, len(friends))

    def first_lower():
        up_copy(0).start()
        own_half(0).start()
        own_half(1).start()

    def first_even():
        to_sibling(0, 0).start()
        to_sibling(0, 7).start()

    pl.when(even)(first_even)
    pl.when(lower)(first_lower)
    pl.when(upper)(lambda: own_x(1).start())
    for cond, plan in ((upper, SEND_UPPER), (lower, SEND_LOWER)):
        def send_first(plan=plan):
            for step in plan[0]:
                own_x(step).start()
        pl.when(cond)(send_first)

    def blank():
        kv[3] = jnp.zeros((KVH, 2, TOK, HD), jnp.bfloat16)
    pl.when(level == 0)(blank)

    for at, (src, wide, dst) in enumerate(((q_rows, wide_o, qh), (g_rows, wide_q, gh))):
        loads[2 + at].wait()
        wide[...] = src[...].astype(jnp.float32)
        for head in range(KVH):
            for r in range(2):
                dst[head, r * TOK:(r + 1) * TOK, :] = (
                    wide[pl.ds(2 * head + r, TOK, stride=16), :].astype(jnp.bfloat16))

    loads[4].wait()
    lengths = []
    for k in range(LEVELS):
        real = lens[jnp.maximum(p - k, 0)]
        lengths.append(jnp.where(level >= k, real, 0))

    def compute(step, blocks):
        head = head_of(step)
        q = qh[head]
        g = gh[head]
        levs = [lax.rem(level - k + LEVELS, LEVELS) for k in range(blocks)]
        key_row = lax.broadcasted_iota(jnp.int32, (TOK, TOK), 0)
        query_tok = lax.broadcasted_iota(jnp.int32, (TOK, TOK), 1)
        floor = jnp.finfo(jnp.float32).min
        keys = jnp.concatenate([kv[lev, head, 0] for lev in levs], axis=0)
        vals = jnp.concatenate([kv[lev, head, 1] for lev in levs], axis=0)
        half_q = [q[r * TOK:(r + 1) * TOK] for r in range(2)]
        half_g = [g[r * TOK:(r + 1) * TOK] for r in range(2)]

        def block(got, k):
            return got[k * TOK:(k + 1) * TOK]

        def softmax(r, scores):
            tops, sums = [], []
            for k in range(blocks):
                seen = key_row < lengths[k]
                if k == 0:
                    seen = seen & (key_row <= query_tok)
                one = jnp.where(seen, block(scores, k) * SCORE_SCALE, -jnp.inf)
                high = jnp.maximum(jnp.max(one, axis=0, keepdims=True), floor)
                expo = jnp.exp2(one - high)
                score[r, k] = expo
                tops.append(high)
                sums.append(jnp.sum(expo, axis=0, keepdims=True))
            top = functools.reduce(jnp.maximum, tops)
            fades = [jnp.exp2(high - top) for high in tops]
            share = 1.0 / sum(one * fade for one, fade in zip(sums, fades))
            factors = [fade * share for fade in fades]
            for k in range(blocks):
                low[r, k] = (score[r, k] * factors[k]).astype(jnp.bfloat16)
            return factors

        def attend(r):
            weights = low[r, 0:blocks].reshape(blocks * TOK, TOK)
            return tn(vals, weights), nn(weights, half_g[r])

        def score_grads(r, out, dw, factors):
            turned = jnp.transpose(half_g[r].astype(jnp.float32))
            row_dot = jnp.sum(out * turned, axis=0, keepdims=True)
            for k in range(blocks):
                slope = (block(dw, k) - row_dot) * factors[k]
                ds[r, k] = (score[r, k] * slope).astype(jnp.bfloat16)

        def back(r):
            slopes = ds[r, 0:blocks].reshape(blocks * TOK, TOK)
            return tn(keys, slopes), nn(slopes, half_q[r])

        def give(r, out, dq):
            wide_o[pl.ds(2 * head + r, TOK, stride=16), :] = jnp.transpose(out)
            wide_q[pl.ds(2 * head + r, TOK, stride=16), :] = jnp.transpose(dq) * SCALE

        factors0 = softmax(0, nt(keys, half_q[0]))
        scores1 = nt(keys, half_q[1])
        out0, dv0 = attend(0)
        factors1 = softmax(1, scores1)
        dw0 = nt(vals, half_g[0])
        out1, dv1 = attend(1)
        score_grads(0, out0, dw0, factors0)
        dw1 = nt(vals, half_g[1])
        dq0, dk0 = back(0)
        score_grads(1, out1, dw1, factors1)
        dq1, dk1 = back(1)
        give(0, out0, dq0)
        give(1, out1, dq1)
        for k in range(blocks):
            for which, got in ((1, block(dv0, k) + block(dv1, k)),
                               (0, (block(dk0, k) + block(dk1, k)) * SCALE)):
                if k % 2 == 0:
                    part[step, k // 2, which] = got
                else:
                    sib_out[step, k // 2, which] = got.astype(jnp.bfloat16)

    def add_sibling(step):
        def add(a, n):
            wait_in(sib_in.at[step, n], sib_sem.at[step, n])
            part[step, a] = part[step, a] + sib_in[step, n].astype(jnp.float32)
        pl.when(even)(lambda: add(0, 0))
        pl.when(level == 3)(lambda: add(1, 0))
        pl.when(level == 2)(lambda: add(1, 1))

    def send_x(step):
        x_out[step] = part[step, 0].astype(jnp.bfloat16)
        x_copy(step).start()

    def finish_upper(step):
        add_sibling(step)
        direct = (step > 0) & (step < 6)
        for via in VIA_X:
            def along_x(via=via):
                x_out_up[STEPS[via][1]] = part[via, 1].astype(jnp.bfloat16)
                x_up_copy(via).start()
            pl.when(step == via)(along_x)
            direct = direct & (step != via)
        pl.when(direct)(lambda: send_down(step))

        def halves():
            for which in range(2):
                y_out[6, which] = part[6, 1, which].astype(jnp.bfloat16)
                down_half(which).start()
        pl.when(step == 6)(halves)
        pl.when((step > 0) & (step < 7))(lambda: send_x(step))

    def send_down(step):
        y_out[step] = part[step, 1].astype(jnp.bfloat16)
        down_copy(step).start()

    def pass_down(at):
        wait_in(x_in_up.at[at], x_up_sem.at[at])
        part[7 * at, 1] = part[7 * at, 1] + x_in_up[at].astype(jnp.float32)
        send_down(7 * at)

    def add_down(step):
        wait_in(y_in.at[step], y_sem.at[step])
        part[step, 0] = part[step, 0] + y_in[step].astype(jnp.float32)

    def take_down(step):
        direct = step > 0
        for via in VIA_X:
            direct = direct & (step != via)
        pl.when(direct)(lambda: add_down(step))
        send_x(step)

    def arrive_same(step):
        def body():
            wait_kv(level, step)
            pl.when(even)(lambda: to_sibling(0, step).start())
        pl.when((step > 0) & (step < 7))(body)

    def arrive_upper(step):
        def below():
            wait_kv(up2, step)
            to_sibling(1, step).start()

        def last_early():
            wait_kv(up2, 7)
            pass_x(VIA_X[1]).start()
            to_sibling(1, 7).start()

        pl.when(step < 7)(below)
        pl.when(step == 0)(lambda: pass_x(VIA_X[0]).start())
        pl.when(step == 1)(last_early)
        arrive_same(step)

    def send_own(step, plan):
        for at, sent in enumerate(plan[1:]):
            def go(sent=sent):
                for one in sent:
                    own_x(one).start()
            pl.when(step == at)(go)

    def step_upper(step):
        send_own(step, SEND_UPPER)
        pl.when(step == 0)(lambda: arrive_upper(step))
        pl.when(step == 2)(lambda: arrive_upper(step))
        pl.when((step > 1) & (step < 6))(lambda: arrive_upper(step + 1))
        pl.when(step > 0)(lambda: finish_upper(step - 1))
        pl.when(step == 5)(lambda: pass_down(0))
        from_sibling(step)
        pl.when(level == 3)(lambda: compute(step, 4))
        pl.when(level == 2)(lambda: compute(step, 3))
        part_copy(0, step).start()
        pl.when(level == 3)(lambda: part_copy(1, step).start())
        pl.when(step == 0)(lambda: arrive_upper(step + 1))

    def step_lower(step):
        send_own(step, SEND_LOWER)
        pl.when(step == 0)(arrive_halves)
        pl.when(step > 1)(lambda: arrive_same(step))
        pl.when((step > 1) & (step < 7) & (step != VIA_X[0]) & (step != VIA_X[1]))(
            lambda: up_copy(step).start())
        pl.when((step > 0) & even)(lambda: add_sibling(step - 1))
        from_sibling(step)
        compute(step, 2)
        pl.when(level == 1)(lambda: part_copy(0, step).start())

    def step_body(step, carry):
        pl.when(upper)(lambda: step_upper(step))
        pl.when(lower)(lambda: step_lower(step))
        return carry

    lax.fori_loop(0, 8, step_body, 0)

    def last_upper():
        finish_upper(jnp.int32(7))
        pass_down(1)

    def last_lower():
        pl.when(even)(lambda: add_sibling(jnp.int32(7)))

        def down_body(step, carry):
            take_down(step)
            return carry
        lax.fori_loop(1, 6, down_body, 0)
        for which in range(2):
            wait_in(y_in.at[6, which], y_sem.at[6 - 4 * which])
            x_out[6, which] = (
                part[6, 0, which] + y_in[6, which].astype(jnp.float32)).astype(jnp.bfloat16)
            x_half(which).start()

    pl.when(upper)(last_upper)
    q_rows[...] = wide_o[...].astype(jnp.bfloat16)
    g_rows[...] = wide_q[...].astype(jnp.bfloat16)
    stores = [
        pltpu.make_async_copy(src, dst, store_sem.at[at])
        for at, (src, dst) in enumerate((
            (q_rows, o_hbm), (g_rows, dq_hbm), (k_rows, dk_hbm), (v_rows, dv_hbm)))
    ]
    stores[0].start()
    stores[1].start()
    pl.when(lower)(last_lower)

    for at in range(2):
        mine = 7 * at
        for step in range(1, 7):
            if STEPS[step][1] == at:
                wait_in(x_in.at[step], x_sem.at[step])
                part[mine, 0] = part[mine, 0] + x_in[step].astype(jnp.float32)
        pl.when(lower)(functools.partial(add_down, mine))
    for which, ref in ((0, k_rows), (1, v_rows)):
        for at in range(2):
            pair[pl.ds(at, TOK, stride=2), :] = part[7 * at, 0, which]
        ref[...] = pair[...].astype(jnp.bfloat16)
        stores[2 + which].start()

    def sent_upper():
        for step in range(1, 7):
            own_x(step).wait_send()
            x_copy(step).wait_send()
        for step in range(8):
            to_sibling(1, step).wait_send()
            part_copy(0, step).wait_send()
        for step in (0, 1, 3, 5, 7):
            down_copy(step).wait_send()
        for which in range(2):
            down_half(which).wait_send()
        for step in VIA_X:
            pass_x(step).wait_send()
            x_up_copy(step).wait_send()

    def sent_lower():
        for step in range(2, 7):
            own_x(step).wait_send()
        for step in range(1, 6):
            x_copy(step).wait_send()
        for which in range(2):
            own_half(which).wait_send()
            up_half(which).wait_send()
            x_half(which).wait_send()
        for step in (0, 3, 5, 6, 7):
            up_copy(step).wait_send()

    pl.when(upper)(sent_upper)
    pl.when(lower)(sent_lower)
    for step in range(8):
        pl.when(even)(lambda step=step: to_sibling(0, step).wait_send())
        pl.when(level == 1)(lambda step=step: part_copy(0, step).wait_send())
        pl.when(level == 3)(lambda step=step: part_copy(1, step).wait_send())
    for store in stores:
        store.wait()


def unload(*refs):
    held, load_sem, store_sem = refs[8:12], refs[12], refs[13]
    moves = []
    for at in range(4):
        rows = refs[at].shape[0] // UNLOADS
        for piece in range(UNLOADS):
            cut = pl.ds(piece * rows, rows)
            moves.append((
                pltpu.make_async_copy(refs[at].at[cut], held[at].at[cut], load_sem.at[at, piece]),
                pltpu.make_async_copy(held[at].at[cut], refs[4 + at].at[cut], store_sem.at[at, piece])))
    for load, _ in moves:
        load.start()
    for load, store in moves:
        load.wait()
        store.start()
    for _, store in moves:
        store.wait()


def shards(queries, keys, values, grad_out, parents, node_lengths):
    del parents
    tokens = queries.shape[0]
    wide_rows = tokens * KVH * 2
    hbm = pl.BlockSpec(memory_space=pltpu.HBM)
    out = pl.pallas_call(
        kernel,
        out_shape=(
            jax.ShapeDtypeStruct((wide_rows, HD), jnp.bfloat16),
            jax.ShapeDtypeStruct((wide_rows, HD), jnp.bfloat16),
            jax.ShapeDtypeStruct((2 * tokens, HD), jnp.bfloat16),
            jax.ShapeDtypeStruct((2 * tokens, HD), jnp.bfloat16),
        ),
        in_specs=[hbm] * 5,
        out_specs=(hbm,) * 4,
        scratch_shapes=[
            pltpu.VMEM((wide_rows, HD), jnp.bfloat16),
            pltpu.VMEM((wide_rows, HD), jnp.bfloat16),
            pltpu.VMEM((2 * tokens, HD), jnp.bfloat16),
            pltpu.VMEM((2 * tokens, HD), jnp.bfloat16),
            pltpu.SMEM(node_lengths.shape, jnp.int32),
            pltpu.VMEM((LEVELS, KVH, 2, TOK, HD), jnp.bfloat16),
            pltpu.VMEM((KVH, ROWS, HD), jnp.bfloat16),
            pltpu.VMEM((KVH, ROWS, HD), jnp.bfloat16),
            pltpu.VMEM((wide_rows, HD), jnp.float32),
            pltpu.VMEM((wide_rows, HD), jnp.float32),
            pltpu.VMEM((2 * tokens, HD), jnp.float32),
            pltpu.VMEM((2, LEVELS, TOK, TOK), jnp.float32),
            pltpu.VMEM((2, LEVELS, TOK, TOK), jnp.bfloat16),
            pltpu.VMEM((2, LEVELS, TOK, TOK), jnp.bfloat16),
            pltpu.VMEM((8, 2, 2, TOK, HD), jnp.float32),
            pltpu.VMEM((8, 2, 2, TOK, HD), jnp.bfloat16),
            pltpu.VMEM((8, 2, 2, TOK, HD), jnp.bfloat16),
            pltpu.VMEM((8, 2, TOK, HD), jnp.bfloat16),
            pltpu.VMEM((8, 2, TOK, HD), jnp.bfloat16),
            pltpu.VMEM((8, 2, TOK, HD), jnp.bfloat16),
            pltpu.VMEM((8, 2, TOK, HD), jnp.bfloat16),
            pltpu.VMEM((2, 2, TOK, HD), jnp.bfloat16),
            pltpu.VMEM((2, 2, TOK, HD), jnp.bfloat16),
            pltpu.SemaphoreType.DMA((5,)),
            pltpu.SemaphoreType.DMA((4,)),
            pltpu.SemaphoreType.DMA((2,)),
            pltpu.SemaphoreType.DMA((LEVELS, 8)),
            pltpu.SemaphoreType.DMA((10, 8)),
            pltpu.SemaphoreType.DMA((8, 2)),
            pltpu.SemaphoreType.DMA((8,)),
            pltpu.SemaphoreType.DMA((2,)),
            pltpu.SemaphoreType.DMA((8,)),
        ],
        compiler_params=pltpu.CompilerParams(
            collective_id=0, has_side_effects=True, vmem_limit_bytes=VMEM_BYTES),
        cost_estimate=pl.CostEstimate(
            flops=12 * 16 * TOK * 4 * TOK * HD, bytes_accessed=5 * 1024 * 1024,
            transcendentals=16 * TOK * 4 * TOK),
    )(
        queries.reshape(wide_rows, HD),
        grad_out.reshape(wide_rows, HD),
        keys.reshape(2 * tokens, HD),
        values.reshape(2 * tokens, HD),
        node_lengths,
    )
    out = pl.pallas_call(
        unload,
        out_shape=tuple(jax.ShapeDtypeStruct(one.shape, one.dtype) for one in out),
        in_specs=[hbm] * 4,
        out_specs=(hbm,) * 4,
        scratch_shapes=[pltpu.VMEM(one.shape, one.dtype) for one in out]
        + [pltpu.SemaphoreType.DMA((4, UNLOADS))] * 2,
        compiler_params=pltpu.CompilerParams(vmem_limit_bytes=VMEM_BYTES),
    )(*out)
    return (
        out[0].reshape(queries.shape),
        out[1].reshape(queries.shape),
        out[2].reshape(keys.shape),
        out[3].reshape(values.shape),
    )


def solution(mesh):
    in_specs = (
        P("node", None, "head", None),
        P("node", "head", None),
        P("node", "head", None),
        P("node", None, "head", None),
        P(),
        P(),
    )
    out_specs = (
        P("node", None, "head", None),
        P("node", None, "head", None),
        P("node", "head", None),
        P("node", "head", None),
    )
    return jax.shard_map(shards, mesh=mesh, in_specs=in_specs, out_specs=out_specs, check_vma=False)
```
